32 devices in a mesh: pipe: 4 (over y, core), expert: 8 (over z, x).
Axes of the slice: x: 2, y: 2, z: 4, core: 2. Of those that a mesh axis runs over, the one named last changes fastest.
Arguments:
- tokens_down: bfloat16 [4, 512, 3072], P('pipe', 'expert'), may hold values from -6 to 6
- cotan_down: bfloat16 [4, 512, 3072], P('pipe', 'expert'), may hold values from -0.59765625 to 0.59765625
- gates_down: bfloat16 [4, 512, 2], P('pipe', 'expert'), may hold values from 0.099609375 to 1
- experts_down: int32 [4, 512, 2], P('pipe', 'expert'), may hold values from 0 to 7, as said below
- tokens_up: bfloat16 [4, 512, 3072], P('pipe', 'expert'), may hold values from -6 to 6
- cotan_up: bfloat16 [4, 512, 3072], P('pipe', 'expert'), may hold values from -0.59765625 to 0.59765625
- gates_up: bfloat16 [4, 512, 2], P('pipe', 'expert'), may hold values from 0.099609375 to 1
- experts_up: int32 [4, 512, 2], P('pipe', 'expert'), may hold values from 0 to 7, as said below
- w_in: bfloat16 [4, 3072, 2048], P('pipe', None, 'expert'), may hold values from -0.109375 to 0.109375
Outputs:
- grad_out: bfloat16 [4, 2048, 3072], P('pipe', 'expert')
The draws below stay inside these ranges and needn't reach their ends.
Inputs may be any that keep to these rules, and one draw needn't show every extreme that they name: `experts_down`: each row names two different experts. In each aligned block of 64 rows (the rows of one device) expert 0 is named by 1 to 17 rows, and by exactly 17 rows in one block of every section. `experts_up`: as for experts_down.
All inputs are finite; a program needn't handle non-finite values.
Results may differ from the reference program's by a relative error of at most 0.0058.
Values may be sent and summed in bfloat16 or wider, within the bound.
No kernel may reach another device: no remote copies, remote signals or barrier semaphores. Data moves between devices by JAX's collectives and lax.ppermute only.
A program may use at most 128 MiB of HBM per device.

```python
import jax
import jax.numpy as jnp
from jax import lax

D = 3072
E = 8
ROWS = 64
CAP = 17
FFW = 2048
N_PIPE = 4
N_EXPERT = 8


def draw_routes(key):
    key_list = jax.random.split(key, 6)
    shape_three = (N_PIPE, N_EXPERT, ROWS)
    counts = jax.random.randint(key_list[0], (N_PIPE, N_EXPERT), 1, CAP + 1)
    full_block = jax.random.randint(key_list[1], (N_PIPE,), 0, N_EXPERT)
    counts = jnp.where(jnp.arange(N_EXPERT)[None, :] == full_block[:, None], CAP, counts)
    scores = jax.random.randint(key_list[2], shape_three, 0, 65536) * ROWS + jnp.arange(ROWS)[None, None, :]
    ordering = jnp.argsort(scores, axis=-1)
    ranking = jnp.argsort(ordering, axis=-1)
    names_zero = ranking < counts[:, :, None]
    first_pick = jax.random.randint(key_list[3], shape_three, 1, E)
    offset_pick = jax.random.randint(key_list[4], shape_three, 1, E - 1)
    second_pick = 1 + (first_pick - 1 + offset_pick) % (E - 1)
    position = jax.random.randint(key_list[5], shape_three, 0, 2)
    left_id = jnp.where(names_zero, jnp.where(position == 0, 0, first_pick), first_pick)
    right_id = jnp.where(names_zero, jnp.where(position == 0, first_pick, 0), second_pick)
    return jnp.stack([left_id, right_id], axis=-1).reshape(N_PIPE, N_EXPERT * ROWS, 2).astype(jnp.int32)


def draw_experts_down(key, part):
    return draw_routes(jax.random.fold_in(key, 11))


def draw_experts_up(key, part):
    return draw_routes(jax.random.fold_in(key, 23))


def block_scale(key, dims, cuts, low, high):
    loudness, own = 1.0, jax.random.fold_in(key, 6)
    for dim, shards_of in cuts:
        draws = jnp.exp(jax.random.uniform(jax.random.fold_in(own, dim), (shards_of,), jnp.float32, low / len(cuts), high / len(cuts)))
        loudness = loudness * jnp.repeat(draws, dims[dim] // shards_of).reshape([-1 if axis == dim else 1 for axis in range(len(dims))])
    return loudness


def scatter_about(stream_key, dims, deviation, bound, pieces=(), held_as=jnp.bfloat16):
    values = deviation * jax.random.normal(stream_key, dims, jnp.float32)
    if pieces:
        values = values * block_scale(stream_key, dims, pieces, -0.22, 0.18)
    return jnp.clip(values, -bound, bound).astype(held_as)


def setup_inputs(seed: int = 0) -> dict:
    seeds = jax.random.split(jax.random.key(seed), 10)
    tokens_down = scatter_about(seeds[0], (N_PIPE, N_EXPERT * ROWS, D), 1.0, 6.0, ((0, 4), (1, 8)))
    cotan_down = scatter_about(seeds[1], (N_PIPE, N_EXPERT * ROWS, D), 0.1, 0.59765625, ((0, 4), (1, 8)))
    gates_down = jnp.clip(0.099609375 + 0.9003906 * jax.random.uniform(seeds[2], (N_PIPE, N_EXPERT * ROWS, 2), jnp.float32) ** block_scale(seeds[2], (N_PIPE, N_EXPERT * ROWS, 2), ((0, 4), (1, 8)), -0.2, 0.2), 0.099609375, 1.0).astype(jnp.bfloat16)
    experts_down = draw_experts_down(jax.random.fold_in(seeds[9], 71), 0)
    tokens_up = scatter_about(seeds[4], (N_PIPE, N_EXPERT * ROWS, D), 1.0, 6.0, ((0, 4), (1, 8)))
    cotan_up = scatter_about(seeds[5], (N_PIPE, N_EXPERT * ROWS, D), 0.1, 0.59765625, ((0, 4), (1, 8)))
    gates_up = jnp.clip(0.099609375 + 0.9003906 * jax.random.uniform(seeds[6], (N_PIPE, N_EXPERT * ROWS, 2), jnp.float32) ** block_scale(seeds[6], (N_PIPE, N_EXPERT * ROWS, 2), ((0, 4), (1, 8)), -0.2, 0.2), 0.099609375, 1.0).astype(jnp.bfloat16)
    experts_up = draw_experts_up(jax.random.fold_in(seeds[9], 71), 0)
    w_in = scatter_about(seeds[8], (N_PIPE, D, FFW), D ** -0.5, 0.109375, ((0, 4), (2, 8)))
    return {"tokens_down": tokens_down, "cotan_down": cotan_down, "gates_down": gates_down, "experts_down": experts_down, "tokens_up": tokens_up, "cotan_up": cotan_up, "gates_up": gates_up, "experts_up": experts_up, "w_in": w_in}


def one_direction(tokens, cotangent, gates, ids, weight_in):
    block_tokens = tokens.reshape(N_EXPERT, ROWS, D)
    block_cotangent = cotangent.reshape(N_EXPERT, ROWS, D)
    is_chosen = ids.reshape(N_EXPERT, ROWS, 2) == 0
    chosen_gate = jnp.sum(jnp.where(is_chosen, gates.reshape(N_EXPERT, ROWS, 2).astype(jnp.float32), jnp.float32(0.0)), axis=-1)
    chosen = jnp.any(is_chosen, axis=-1)
    slots_of = jnp.cumsum(chosen.astype(jnp.int32), axis=1).astype(jnp.int32) - 1
    slots_of = jnp.where(chosen, slots_of, jnp.int32(CAP)).astype(jnp.int32)
    source = jnp.broadcast_to(jnp.arange(N_EXPERT, dtype=jnp.int32)[:, None], (N_EXPERT, ROWS))
    scaled = (chosen_gate[..., None] * block_cotangent.astype(jnp.float32)).astype(jnp.bfloat16)
    slot_tokens = jnp.zeros((N_EXPERT, CAP, D), jnp.bfloat16).at[source, slots_of].set(block_tokens, mode="drop")
    slot_scaled = jnp.zeros((N_EXPERT, CAP, D), jnp.bfloat16).at[source, slots_of].set(scaled, mode="drop")
    rows_x = slot_tokens.reshape(N_EXPERT * CAP, D)
    rows_y = slot_scaled.reshape(N_EXPERT * CAP, D)
    hidden = jnp.dot(rows_x, weight_in, preferred_element_type=jnp.float32)
    active = (hidden * jax.nn.sigmoid(hidden)).astype(jnp.bfloat16)
    return lax.dot_general(active, rows_y, (((0,), (0,)), ((), ())), preferred_element_type=jnp.float32)


def one_layer(layer_args):
    tok_dn, cot_dn, gate_dn, ids_dn, tok_up, cot_up, gate_up, ids_up, weight_in = layer_args
    summed = one_direction(tok_dn, cot_dn, gate_dn, ids_dn, weight_in) + one_direction(tok_up, cot_up, gate_up, ids_up, weight_in)
    return summed.astype(jnp.bfloat16)


def reference(tokens_down, cotan_down, gates_down, experts_down, tokens_up, cotan_up, gates_up, experts_up, w_in):
    return lax.map(one_layer, (tokens_down, cotan_down, gates_down, experts_down,
                               tokens_up[::-1], cotan_up[::-1], gates_up[::-1], experts_up[::-1], w_in))
```

```python
import functools

import jax
import jax.numpy as jnp
from jax import lax
from jax.experimental import pallas as pl
from jax.experimental.pallas import tpu as pltpu
from jax.sharding import PartitionSpec as P

CAP = 17
MAIN = 16
SEGS = 8


def grid_cycle(n):
    fast = 1
    while 4 * fast * fast <= n:
        fast *= 2
    slow = n // fast
    order = [s * fast for s in range(slow)]
    for s in reversed(range(slow)):
        columns = range(1, fast)
        if (slow - 1 - s) % 2 == 1:
            columns = reversed(columns)
        order += [s * fast + c for c in columns]
    return order


def pack_kernel(tokens_ref, cotan_ref, gates_ref, ids_ref, out_ref):
    rows, width = tokens_ref.shape
    named = ids_ref[...] == 0
    picked = jnp.where(named, gates_ref[...].astype(jnp.float32), 0.0)
    gate = jnp.sum(picked, axis=0, keepdims=True)
    chosen = jnp.sum(named.astype(jnp.float32), axis=0, keepdims=True)
    earlier = (
        lax.broadcasted_iota(jnp.int32, (rows, rows), 0)
        < lax.broadcasted_iota(jnp.int32, (rows, rows), 1)
    ).astype(jnp.float32)
    slot = jnp.dot(
        jnp.broadcast_to(chosen, (8, rows)), earlier, preferred_element_type=jnp.float32
    )[:1]
    slot = slot.astype(jnp.int32)
    want = lax.broadcasted_iota(jnp.int32, (2 * MAIN, rows), 0)
    hit = (want == slot) & (chosen > 0.0) & (want < CAP)
    placing = hit.astype(jnp.bfloat16)
    slot_gate = jnp.sum(jnp.where(hit, gate, 0.0), axis=1, keepdims=True)
    x = jnp.dot(placing, tokens_ref[...], preferred_element_type=jnp.float32)
    y = jnp.dot(placing, cotan_ref[...], preferred_element_type=jnp.float32) * slot_gate
    seg = width // SEGS
    out_ref[:, :width] = x[:MAIN].astype(jnp.bfloat16)
    out_ref[:, width : 2 * width] = y[:MAIN].astype(jnp.bfloat16)
    tail = [x[MAIN : MAIN + 1, s * seg : (s + 1) * seg] for s in range(SEGS)]
    tail += [y[MAIN : MAIN + 1, s * seg : (s + 1) * seg] for s in range(SEGS)]
    out_ref[:, 2 * width :] = jnp.concatenate(tail, axis=0).astype(jnp.bfloat16)


def pack(tokens, cotan, gates, ids):
    rows, width = tokens.shape
    seg = width // SEGS
    return pl.pallas_call(
        pack_kernel,
        out_shape=jax.ShapeDtypeStruct((MAIN, 2 * width + seg), jnp.bfloat16),
        in_specs=[pl.BlockSpec(memory_space=pltpu.VMEM)] * 4,
        out_specs=pl.BlockSpec(memory_space=pltpu.VMEM),
        compiler_params=pltpu.CompilerParams(vmem_limit_bytes=16 * 2**20),
        cost_estimate=pl.CostEstimate(
            flops=4 * 2 * MAIN * rows * width, bytes_accessed=6 * rows * width, transcendentals=0
        ),
        name="pack_slots",
    )(tokens, cotan, gates.T, ids.T)


def grad_kernel(count, *refs):
    payloads, w_ref, out_ref = refs[:count], refs[count], refs[count + 1]
    width = w_ref.shape[0]
    seg = width // SEGS
    size = count * 2 * SEGS
    tails = jnp.concatenate([p[:, 2 * width :] for p in payloads], axis=0)
    row = lax.broadcasted_iota(jnp.int32, (size, size), 0)
    col = lax.broadcasted_iota(jnp.int32, (size, size), 1)
    order = ((row % count) * (2 * SEGS) + row // count == col).astype(jnp.bfloat16)
    tails = jnp.dot(order, tails, preferred_element_type=jnp.float32).astype(jnp.bfloat16)
    x_tail = jnp.concatenate(
        [tails[s * count : (s + 1) * count] for s in range(SEGS)], axis=1
    )
    y_tail = jnp.concatenate(
        [tails[(SEGS + s) * count : (SEGS + s + 1) * count] for s in range(SEGS)], axis=1
    )
    rows_x = jnp.concatenate([p[:, :width] for p in payloads] + [x_tail], axis=0)
    hidden = jnp.dot(rows_x, w_ref[...], preferred_element_type=jnp.float32)
    active = (hidden * jax.nn.sigmoid(hidden)).astype(jnp.bfloat16)
    for s in range(SEGS):
        cut = slice(width + s * seg, width + (s + 1) * seg)
        rows_y = jnp.concatenate(
            [p[:, cut] for p in payloads] + [y_tail[:, s * seg : (s + 1) * seg]], axis=0
        )
        out_ref[:, s * seg : (s + 1) * seg] = lax.dot_general(
            active, rows_y, (((0,), (0,)), ((), ())), preferred_element_type=jnp.float32
        ).astype(jnp.bfloat16)


def grad(payloads, weight_in):
    width, hidden = weight_in.shape
    count = len(payloads)
    return pl.pallas_call(
        functools.partial(grad_kernel, count),
        out_shape=jax.ShapeDtypeStruct((hidden, width), jnp.bfloat16),
        in_specs=[pl.BlockSpec(memory_space=pltpu.VMEM)] * (count + 1),
        out_specs=pl.BlockSpec(memory_space=pltpu.VMEM),
        compiler_params=pltpu.CompilerParams(vmem_limit_bytes=48 * 2**20),
        cost_estimate=pl.CostEstimate(
            flops=4 * CAP * count * width * hidden,
            bytes_accessed=4 * width * hidden,
            transcendentals=CAP * count * hidden,
        ),
        name="grad_of_slots",
    )(*payloads, weight_in)


def ring(block, right_steps, left_steps, cycle):
    n = len(cycle)
    right = [(cycle[i], cycle[(i + 1) % n]) for i in range(n)]
    left = [(b, a) for a, b in right]
    got, going_right, going_left = [block], block, block
    for step in range(max(right_steps, left_steps)):
        if step < right_steps:
            going_right = lax.ppermute(going_right, "expert", right)
            got.append(going_right)
        if step < left_steps:
            going_left = lax.ppermute(going_left, "expert", left)
            got.append(going_left)
    return got


def body(
    tokens_down,
    cotan_down,
    gates_down,
    experts_down,
    tokens_up,
    cotan_up,
    gates_up,
    experts_up,
    w_in,
):
    n_pipe, n_expert = lax.axis_size("pipe"), lax.axis_size("expert")
    up = pack(tokens_up[0], cotan_up[0], gates_up[0], experts_up[0])
    down = pack(tokens_down[0], cotan_down[0], gates_down[0], experts_down[0])
    up = lax.ppermute(up, "pipe", [(i, n_pipe - 1 - i) for i in range(n_pipe)])
    cycle = grid_cycle(n_expert)
    short = (n_expert - 1) // 2
    long = n_expert - 1 - short
    got = ring(down, long, short, cycle) + ring(up, short, long, cycle)
    return grad(got, w_in[0])[None]


def solution(mesh):
    rows = P("pipe", "expert", None)
    in_specs = (rows,) * 8 + (P("pipe", None, "expert"),)
    return jax.shard_map(body, mesh=mesh, in_specs=in_specs, out_specs=rows, check_vma=False)
```

```python
import functools

import jax
import jax.numpy as jnp
from jax import lax
from jax.experimental import pallas as pl
from jax.experimental.pallas import tpu as pltpu
from jax.sharding import PartitionSpec as P

CAP = 17
MAIN = 16
SEGS = 8


def grid_cycle(n):
    fast = 1
    while 4 * fast * fast <= n:
        fast *= 2
    slow = n // fast
    order = [s * fast for s in range(slow)]
    for s in reversed(range(slow)):
        columns = range(1, fast)
        if (slow - 1 - s) % 2 == 1:
            columns = reversed(columns)
        order += [s * fast + c for c in columns]
    return order


def place(gates, ids):
    rows = ids.shape[1]
    named = ids == 0
    gate = jnp.sum(jnp.where(named, gates.astype(jnp.float32), 0.0), axis=0, keepdims=True)
    chosen = jnp.sum(named.astype(jnp.float32), axis=0, keepdims=True)
    earlier = (
        lax.broadcasted_iota(jnp.int32, (rows, rows), 0)
        < lax.broadcasted_iota(jnp.int32, (rows, rows), 1)
    ).astype(jnp.float32)
    slot = jnp.dot(
        jnp.broadcast_to(chosen, (8, rows)), earlier, preferred_element_type=jnp.float32
    )[:1].astype(jnp.int32)
    want = lax.broadcasted_iota(jnp.int32, (2 * MAIN, rows), 0)
    hit = (want == slot) & (chosen > 0.0) & (want < CAP)
    slot_gate = jnp.sum(jnp.where(hit, gate, 0.0), axis=1, keepdims=True)
    return hit.astype(jnp.bfloat16), slot_gate


def pack_kernel(*refs):
    hbm, outs, held, sems = refs[:8], refs[8:10], refs[10:18], refs[18]
    order = [2, 3, 6, 7, 4, 5, 0, 1]
    copies = {i: pltpu.make_async_copy(hbm[i], held[i], sems.at[i]) for i in order}
    for i in order:
        copies[i].start()
    for i in order[:4]:
        copies[i].wait()
    places = [place(held[d + 2][...], held[d + 3][...]) for d in (0, 4)]
    for d, (placing, slot_gate), out_ref in ((4, places[1], outs[1]), (0, places[0], outs[0])):
        copies[d].wait()
        copies[d + 1].wait()
        width = held[d].shape[1]
        seg = width // SEGS
        x = jnp.dot(placing, held[d][...], preferred_element_type=jnp.float32)
        y = jnp.dot(placing, held[d + 1][...], preferred_element_type=jnp.float32) * slot_gate
        out_ref[:, :width] = x[:MAIN].astype(jnp.bfloat16)
        out_ref[:, width : 2 * width] = y[:MAIN].astype(jnp.bfloat16)
        tail = [x[MAIN : MAIN + 1, s * seg : (s + 1) * seg] for s in range(SEGS)]
        tail += [y[MAIN : MAIN + 1, s * seg : (s + 1) * seg] for s in range(SEGS)]
        out_ref[:, 2 * width :] = jnp.concatenate(tail, axis=0).astype(jnp.bfloat16)


def pack(arrays):
    rows, width = arrays[0].shape
    seg = width // SEGS
    payload = jax.ShapeDtypeStruct((MAIN, 2 * width + seg), jnp.bfloat16)
    return pl.pallas_call(
        pack_kernel,
        out_shape=(payload, payload),
        in_specs=[pl.BlockSpec(memory_space=pltpu.HBM)] * 8,
        out_specs=(pl.BlockSpec(memory_space=pltpu.VMEM),) * 2,
        scratch_shapes=[pltpu.VMEM(a.shape, a.dtype) for a in arrays]
        + [pltpu.SemaphoreType.DMA((8,))],
        compiler_params=pltpu.CompilerParams(vmem_limit_bytes=60 * 2**20),
        cost_estimate=pl.CostEstimate(
            flops=8 * 2 * MAIN * rows * width, bytes_accessed=12 * rows * width, transcendentals=0
        ),
        name="pack_slots",
    )(*arrays)


class Block:
    def __init__(self, width, first, second=None):
        self.width, self.first, self.second = width, first, second

    def __getitem__(self, where):
        rows, lanes = where
        if self.second is None:
            return self.first[rows, lanes]
        if lanes.stop is not None and lanes.stop <= self.width:
            return self.first[rows, lanes]
        stop = lanes.stop if lanes.stop is None else lanes.stop - self.width
        return self.second[rows, lanes.start - self.width : stop]


def grad_kernel(count, last, *refs):
    blocks, refs = refs[: count + 1], refs[count + 1 :]
    w_ref, refs = refs[0], refs[1:]
    width = w_ref.shape[0]
    payloads = [Block(width, b) for b in blocks[: count - 1]] + [Block(width, *blocks[count - 1 :])]
    seg = width // SEGS
    size = count * 2 * SEGS
    tails = jnp.concatenate([p[:, 2 * width :] for p in payloads], axis=0)
    row = lax.broadcasted_iota(jnp.int32, (size, size), 0)
    col = lax.broadcasted_iota(jnp.int32, (size, size), 1)
    order = ((row % count) * (2 * SEGS) + row // count == col).astype(jnp.bfloat16)
    tails = jnp.dot(order, tails, preferred_element_type=jnp.float32)
    x_tail = jnp.concatenate(
        [tails[s * count : (s + 1) * count] for s in range(SEGS)], axis=1
    ).astype(jnp.bfloat16)
    y_tail = jnp.concatenate(
        [tails[(SEGS + s) * count : (SEGS + s + 1) * count] for s in range(SEGS)], axis=1
    ).astype(jnp.bfloat16)
    rows_x = jnp.concatenate([p[:, :width] for p in payloads] + [x_tail], axis=0)
    hidden = jnp.dot(rows_x, w_ref[...], preferred_element_type=jnp.float32)
    active = (hidden * jax.nn.sigmoid(hidden)).astype(jnp.bfloat16)
    if last:
        before, out_ref, made, sems = refs
    else:
        (out_ref,) = refs
    copies = []
    for s in range(SEGS):
        cut = slice(width + s * seg, width + (s + 1) * seg)
        here = slice(s * seg, (s + 1) * seg)
        rows_y = jnp.concatenate([p[:, cut] for p in payloads] + [y_tail[:, here]], axis=0)
        part = lax.dot_general(
            active, rows_y, (((0,), (0,)), ((), ())), preferred_element_type=jnp.float32
        )
        if not last:
            out_ref[:, here] = part
            continue
        made[:, here] = (before[:, here] + part).astype(jnp.bfloat16)
        copies.append(
            pltpu.make_async_copy(made.at[:, here], out_ref.at[:, here], sems.at[s])
        )
        copies[-1].start()
    for copy in copies:
        copy.wait()


def grad(payloads, weight_in, before=None, flops=0):
    width, hidden = weight_in.shape
    count = len(payloads) - 1
    last = before is not None
    operands = (*payloads, weight_in) + ((before,) if last else ())
    return pl.pallas_call(
        functools.partial(grad_kernel, count, last),
        out_shape=jax.ShapeDtypeStruct((hidden, width), jnp.bfloat16 if last else jnp.float32),
        in_specs=[pl.BlockSpec(memory_space=pltpu.VMEM)] * len(operands),
        out_specs=pl.BlockSpec(memory_space=pltpu.HBM if last else pltpu.VMEM),
        scratch_shapes=[
            pltpu.VMEM((hidden, width), jnp.bfloat16),
            pltpu.SemaphoreType.DMA((SEGS,)),
        ]
        if last
        else [],
        compiler_params=pltpu.CompilerParams(vmem_limit_bytes=40 * 2**20),
        cost_estimate=pl.CostEstimate(
            flops=flops or 4 * CAP * count * width * hidden,
            bytes_accessed=4 * width * hidden,
            transcendentals=CAP * count * hidden,
        ),
        name="grad_sum" if last else "grad_part",
    )(*operands)


def gather_both(down, up, n_pipe, cycle, width):
    n = len(cycle)
    right = [(cycle[i], cycle[(i + 1) % n]) for i in range(n)]
    left = [(b, a) for a, b in right]
    full = (n - 1) // 2

    def step(pair):
        return (
            lax.ppermute(pair[0], "expert", right),
            lax.ppermute(pair[1], "expert", left),
        )

    def mirrored(block, moves):
        pairs = [(p * n + a, (n_pipe - 1 - p) * n + b) for p in range(n_pipe) for a, b in moves]
        return lax.ppermute(block, ("pipe", "expert"), pairs)

    down_pair = step((down, down))
    up_pair = (mirrored(up, right), mirrored(up, left))
    got_down = [down, *down_pair]
    got_up = [mirrored(up, [(e, e) for e in range(n)]), *up_pair]
    for _ in range(1, full):
        down_pair = step(down_pair)
        got_down += down_pair
        up_pair = step(up_pair)
        got_up += up_pair
    down_pair = step((down_pair[0][:, :width], down_pair[1][:, width:]))
    up_pair = step((up_pair[0][:, :width], up_pair[1][:, width:]))
    return got_down + list(down_pair), got_up + list(up_pair)


def body(
    tokens_down,
    cotan_down,
    gates_down,
    experts_down,
    tokens_up,
    cotan_up,
    gates_up,
    experts_up,
    w_in,
):
    n_pipe, n_expert = lax.axis_size("pipe"), lax.axis_size("expert")
    down, up = pack(
        (
            *(tokens_down[0], cotan_down[0], gates_down[0].T, experts_down[0].T),
            *(tokens_up[0], cotan_up[0], gates_up[0].T, experts_up[0].T),
        )
    )
    got_down, got_up = gather_both(down, up, n_pipe, grid_cycle(n_expert), w_in.shape[1])
    part = grad(got_down, w_in[0])
    return grad(got_up, w_in[0], part)[None]


def solution(mesh):
    rows = P("pipe", "expert", None)
    in_specs = (rows,) * 8 + (P("pipe", None, "expert"),)
    return jax.shard_map(body, mesh=mesh, in_specs=in_specs, out_specs=rows, check_vma=False)
```

```python
import functools

import jax
import jax.numpy as jnp
from jax import lax
from jax.experimental import pallas as pl
from jax.experimental.pallas import tpu as pltpu
from jax.sharding import PartitionSpec as P

CAP = 17
MAIN = 16
SEGS = 8


def grid_cycle(n):
    fast = 1
    while 4 * fast * fast <= n:
        fast *= 2
    slow = n // fast
    order = [s * fast for s in range(slow)]
    for s in reversed(range(slow)):
        columns = range(1, fast)
        if (slow - 1 - s) % 2 == 1:
            columns = reversed(columns)
        order += [s * fast + c for c in columns]
    return order


def place(gates, ids):
    rows = ids.shape[1]
    named = ids == 0
    gate = jnp.sum(jnp.where(named, gates.astype(jnp.float32), 0.0), axis=0, keepdims=True)
    chosen = jnp.sum(named.astype(jnp.float32), axis=0, keepdims=True)
    earlier = (
        lax.broadcasted_iota(jnp.int32, (rows, rows), 0)
        < lax.broadcasted_iota(jnp.int32, (rows, rows), 1)
    ).astype(jnp.float32)
    slot = jnp.dot(
        jnp.broadcast_to(chosen, (8, rows)), earlier, preferred_element_type=jnp.float32
    )[:1].astype(jnp.int32)
    want = lax.broadcasted_iota(jnp.int32, (2 * MAIN, rows), 0)
    hit = (want == slot) & (chosen > 0.0) & (want < CAP)
    slot_gate = jnp.sum(jnp.where(hit, gate, 0.0), axis=1, keepdims=True)
    return hit.astype(jnp.bfloat16), slot_gate


def pack_kernel(*refs):
    hbm, outs, held, sems = refs[:8], refs[8:10], refs[10:18], refs[18]
    order = [2, 3, 6, 7, 4, 5, 0, 1]
    copies = {i: pltpu.make_async_copy(hbm[i], held[i], sems.at[i]) for i in order}
    for i in order:
        copies[i].start()
    for i in order[:4]:
        copies[i].wait()
    places = [place(held[d + 2][...], held[d + 3][...]) for d in (0, 4)]
    for d, (placing, slot_gate), out_ref in ((4, places[1], outs[1]), (0, places[0], outs[0])):
        copies[d].wait()
        copies[d + 1].wait()
        width = held[d].shape[1]
        seg = width // SEGS
        x = jnp.dot(placing, held[d][...], preferred_element_type=jnp.float32)
        y = jnp.dot(placing, held[d + 1][...], preferred_element_type=jnp.float32) * slot_gate
        out_ref[:, :width] = x[:MAIN].astype(jnp.bfloat16)
        out_ref[:, width : 2 * width] = y[:MAIN].astype(jnp.bfloat16)
        tail = [x[MAIN : MAIN + 1, s * seg : (s + 1) * seg] for s in range(SEGS)]
        tail += [y[MAIN : MAIN + 1, s * seg : (s + 1) * seg] for s in range(SEGS)]
        out_ref[:, 2 * width :] = jnp.concatenate(tail, axis=0).astype(jnp.bfloat16)


def pack(arrays):
    rows, width = arrays[0].shape
    seg = width // SEGS
    payload = pltpu.VMEM((MAIN, 2 * width + seg), jnp.bfloat16)
    arrays = [pltpu.with_memory_space_constraint(a, pltpu.HBM) for a in arrays]
    return pl.pallas_call(
        pack_kernel,
        out_shape=(payload, payload),
        in_specs=[pl.BlockSpec(memory_space=pltpu.HBM)] * 8,
        out_specs=(pl.BlockSpec(memory_space=pltpu.VMEM),) * 2,
        scratch_shapes=[pltpu.VMEM(a.shape, a.dtype) for a in arrays]
        + [pltpu.SemaphoreType.DMA((8,))],
        compiler_params=pltpu.CompilerParams(vmem_limit_bytes=16 * 2**20),
        cost_estimate=pl.CostEstimate(
            flops=8 * 2 * MAIN * rows * width, bytes_accessed=12 * rows * width, transcendentals=0
        ),
        name="pack_slots",
    )(*arrays)


def grad_kernel(count, last, *refs):
    payloads, w_ref, refs = refs[:count], refs[count], refs[count + 1 :]
    width = w_ref.shape[0]
    seg = width // SEGS
    size = count * 2 * SEGS
    tails = jnp.concatenate([p[:, 2 * width :] for p in payloads], axis=0)
    row = lax.broadcasted_iota(jnp.int32, (size, size), 0)
    col = lax.broadcasted_iota(jnp.int32, (size, size), 1)
    order = ((row % count) * (2 * SEGS) + row // count == col).astype(jnp.bfloat16)
    tails = jnp.dot(order, tails, preferred_element_type=jnp.float32)
    x_tail = jnp.concatenate(
        [tails[s * count : (s + 1) * count] for s in range(SEGS)], axis=1
    ).astype(jnp.bfloat16)
    y_tail = jnp.concatenate(
        [tails[(SEGS + s) * count : (SEGS + s + 1) * count] for s in range(SEGS)], axis=1
    ).astype(jnp.bfloat16)
    rows_x = jnp.concatenate([p[:, :width] for p in payloads] + [x_tail], axis=0)
    hidden = jnp.dot(rows_x, w_ref[...], preferred_element_type=jnp.float32)
    active = (hidden * jax.nn.sigmoid(hidden)).astype(jnp.bfloat16)
    if last:
        before, out_ref, made, sems = refs
    else:
        (out_ref,) = refs
    copies = []
    for s in range(SEGS):
        cut = slice(width + s * seg, width + (s + 1) * seg)
        here = slice(s * seg, (s + 1) * seg)
        rows_y = jnp.concatenate([p[:, cut] for p in payloads] + [y_tail[:, here]], axis=0)
        part = lax.dot_general(
            active, rows_y, (((0,), (0,)), ((), ())), preferred_element_type=jnp.float32
        )
        if not last:
            out_ref[:, here] = part
            continue
        made[:, here] = (before[:, here] + part).astype(jnp.bfloat16)
        copies.append(
            pltpu.make_async_copy(made.at[:, here], out_ref.at[:, here], sems.at[s])
        )
        copies[-1].start()
    for copy in copies:
        copy.wait()


def grad(payloads, weight_in, before=None):
    width, hidden = weight_in.shape
    count = len(payloads)
    last = before is not None
    operands = (*payloads, weight_in) + ((before,) if last else ())
    return pl.pallas_call(
        functools.partial(grad_kernel, count, last),
        out_shape=jax.ShapeDtypeStruct((hidden, width), jnp.bfloat16 if last else jnp.float32),
        in_specs=[pl.BlockSpec(memory_space=pltpu.VMEM)] * len(operands),
        out_specs=pl.BlockSpec(memory_space=pltpu.HBM if last else pltpu.VMEM),
        scratch_shapes=[
            pltpu.VMEM((hidden, width), jnp.bfloat16),
            pltpu.SemaphoreType.DMA((SEGS,)),
        ]
        if last
        else [],
        compiler_params=pltpu.CompilerParams(vmem_limit_bytes=40 * 2**20),
        cost_estimate=pl.CostEstimate(
            flops=4 * CAP * count * width * hidden,
            bytes_accessed=4 * width * hidden,
            transcendentals=CAP * count * hidden,
        ),
        name="grad_sum" if last else "grad_part",
    )(*operands)


def gather_both(down, up, n_pipe, cycle):
    n = len(cycle)
    right = [(cycle[i], cycle[(i + 1) % n]) for i in range(n)]
    left = [(b, a) for a, b in right]

    def mirrored(block, moves):
        pairs = [(p * n + a, (n_pipe - 1 - p) * n + b) for p in range(n_pipe) for a, b in moves]
        return lax.ppermute(block, ("pipe", "expert"), pairs)

    def turn(at):
        up_left, down_right, up_right, down_left = at
        return (
            lax.ppermute(up_left, "expert", left),
            lax.ppermute(down_right, "expert", right),
            lax.ppermute(up_right, "expert", right),
            lax.ppermute(down_left, "expert", left),
        )

    at = (
        mirrored(up, left),
        lax.ppermute(down, "expert", right),
        mirrored(up, right),
        lax.ppermute(down, "expert", left),
    )
    got = [*at]
    for _ in range(1, (n - 1) // 2):
        at = turn(at)
        got += at
    last = (lax.ppermute(at[0], "expert", left), lax.ppermute(at[1], "expert", right))
    own = mirrored(up, [(e, e) for e in range(n)])
    return [*reversed(got), own, down], last


def body(
    tokens_down,
    cotan_down,
    gates_down,
    experts_down,
    tokens_up,
    cotan_up,
    gates_up,
    experts_up,
    w_in,
):
    n_pipe, n_expert = lax.axis_size("pipe"), lax.axis_size("expert")
    down, up = pack(
        (
            *(tokens_down[0], cotan_down[0], gates_down[0].T, experts_down[0].T),
            *(tokens_up[0], cotan_up[0], gates_up[0].T, experts_up[0].T),
        )
    )
    got, last = gather_both(down, up, n_pipe, grid_cycle(n_expert))
    part = grad(got, w_in[0])
    return grad(last, w_in[0], part)[None]


def solution(mesh):
    rows = P("pipe", "expert", None)
    in_specs = (rows,) * 8 + (P("pipe", None, "expert"),)
    return jax.shard_map(body, mesh=mesh, in_specs=in_specs, out_specs=rows, check_vma=False)
```

```python
import functools

import jax
import jax.numpy as jnp
from jax import lax
from jax.experimental import pallas as pl
from jax.experimental.pallas import tpu as pltpu
from jax.sharding import PartitionSpec as P

CAP = 17
MAIN = 16
SEGS = 8


def grid_cycle(n):
    fast = 1
    while 4 * fast * fast <= n:
        fast *= 2
    slow = n // fast
    order = [s * fast for s in range(slow)]
    for s in reversed(range(slow)):
        columns = range(1, fast)
        if (slow - 1 - s) % 2 == 1:
            columns = reversed(columns)
        order += [s * fast + c for c in columns]
    return order


def place(gates, ids):
    rows = ids.shape[1]
    named = ids == 0
    gate = jnp.sum(jnp.where(named, gates.astype(jnp.float32), 0.0), axis=0, keepdims=True)
    chosen = jnp.sum(named.astype(jnp.float32), axis=0, keepdims=True)
    earlier = (
        lax.broadcasted_iota(jnp.int32, (rows, rows), 0)
        < lax.broadcasted_iota(jnp.int32, (rows, rows), 1)
    ).astype(jnp.float32)
    slot = jnp.dot(
        jnp.broadcast_to(chosen, (8, rows)), earlier, preferred_element_type=jnp.float32
    )[:1].astype(jnp.int32)
    want = lax.broadcasted_iota(jnp.int32, (2 * MAIN, rows), 0)
    hit = (want == slot) & (chosen > 0.0) & (want < CAP)
    slot_gate = jnp.sum(jnp.where(hit, gate, 0.0), axis=1, keepdims=True)
    return hit.astype(jnp.bfloat16), slot_gate


def pack_kernel(*refs):
    hbm, outs, held, sems = refs[:8], refs[8:10], refs[10:18], refs[18]
    order = [2, 3, 6, 7, 4, 5, 0, 1]
    copies = {i: pltpu.make_async_copy(hbm[i], held[i], sems.at[i]) for i in order}
    for i in order:
        copies[i].start()
    for i in order[:4]:
        copies[i].wait()
    places = [place(held[d + 2][...], held[d + 3][...]) for d in (0, 4)]
    for d, (placing, slot_gate), out_ref in ((4, places[1], outs[1]), (0, places[0], outs[0])):
        copies[d].wait()
        copies[d + 1].wait()
        width = held[d].shape[1]
        seg = width // SEGS
        x = jnp.dot(placing, held[d][...], preferred_element_type=jnp.float32)
        y = jnp.dot(placing, held[d + 1][...], preferred_element_type=jnp.float32) * slot_gate
        out_ref[:, :width] = x[:MAIN].astype(jnp.bfloat16)
        out_ref[:, width + seg :] = y[:MAIN].astype(jnp.bfloat16)
        tail = [x[MAIN : MAIN + 1, s * seg : (s + 1) * seg] for s in range(SEGS)]
        tail += [y[MAIN : MAIN + 1, s * seg : (s + 1) * seg] for s in range(SEGS)]
        out_ref[:, width : width + seg] = jnp.concatenate(tail, axis=0).astype(jnp.bfloat16)


def pack(arrays):
    rows, width = arrays[0].shape
    seg = width // SEGS
    payload = pltpu.VMEM((MAIN, 2 * width + seg), jnp.bfloat16)
    arrays = [pltpu.with_memory_space_constraint(a, pltpu.HBM) for a in arrays]
    return pl.pallas_call(
        pack_kernel,
        out_shape=(payload, payload),
        in_specs=[pl.BlockSpec(memory_space=pltpu.HBM)] * 8,
        out_specs=(pl.BlockSpec(memory_space=pltpu.VMEM),) * 2,
        scratch_shapes=[pltpu.VMEM(a.shape, a.dtype) for a in arrays]
        + [pltpu.SemaphoreType.DMA((8,))],
        compiler_params=pltpu.CompilerParams(vmem_limit_bytes=16 * 2**20),
        cost_estimate=pl.CostEstimate(
            flops=8 * 2 * MAIN * rows * width, bytes_accessed=12 * rows * width, transcendentals=0
        ),
        name="pack_slots",
    )(*arrays)


def activate(payloads, w_ref):
    count, width = len(payloads), w_ref.shape[0]
    seg = width // SEGS
    size = count * 2 * SEGS
    tails = jnp.concatenate([p[:, width : width + seg] for p in payloads], axis=0)
    row = lax.broadcasted_iota(jnp.int32, (size, size), 0)
    col = lax.broadcasted_iota(jnp.int32, (size, size), 1)
    order = ((row % count) * (2 * SEGS) + row // count == col).astype(jnp.bfloat16)
    tails = jnp.dot(order, tails, preferred_element_type=jnp.float32)
    x_tail, y_tail = (
        jnp.concatenate(
            [tails[s * count : (s + 1) * count] for s in range(first, first + SEGS)], axis=1
        ).astype(jnp.bfloat16)
        for first in (0, SEGS)
    )
    rows_x = jnp.concatenate([p[:, :width] for p in payloads] + [x_tail], axis=0)
    hidden = jnp.dot(rows_x, w_ref[...], preferred_element_type=jnp.float32)
    return (hidden * jax.nn.sigmoid(hidden)).astype(jnp.bfloat16), y_tail


def times(active, rows_y):
    return lax.dot_general(
        active, rows_y, (((0,), (0,)), ((), ())), preferred_element_type=jnp.float32
    )


def part_kernel(count, *refs):
    payloads, (w_ref, out_ref) = refs[:count], refs[count:]
    width = w_ref.shape[0]
    seg = width // SEGS
    active, y_tail = activate(payloads, w_ref)
    for s in range(SEGS):
        here = slice(s * seg, (s + 1) * seg)
        there = slice(width + (s + 1) * seg, width + (s + 2) * seg)
        rows_y = jnp.concatenate([p[:, there] for p in payloads] + [y_tail[:, here]], axis=0)
        out_ref[:, here] = times(active, rows_y)


def active_kernel(count, *refs):
    payloads, (w_ref, active_ref, tail_ref) = refs[:count], refs[count:]
    active_ref[...], tail_ref[...] = activate(payloads, w_ref)


def sum_kernel(count, *refs):
    blocks, (active_ref, tail_ref, before, out_ref, made, sems) = refs[:count], refs[count:]
    seg = tail_ref.shape[1] // SEGS
    active = active_ref[...]
    copies = []
    for s in range(SEGS):
        here = slice(s * seg, (s + 1) * seg)
        rows_y = jnp.concatenate([b[:, here] for b in blocks] + [tail_ref[:, here]], axis=0)
        made[:, here] = (before[:, here] + times(active, rows_y)).astype(jnp.bfloat16)
        copies.append(
            pltpu.make_async_copy(made.at[:, here], out_ref.at[:, here], sems.at[s])
        )
        copies[-1].start()
    for copy in copies:
        copy.wait()


def local_call(kernel, name, operands, outs, scratch=(), flops=0):
    specs = tuple(
        pl.BlockSpec(
            memory_space=pltpu.HBM if isinstance(out, jax.ShapeDtypeStruct) else pltpu.VMEM
        )
        for out in outs
    )
    return pl.pallas_call(
        kernel,
        out_shape=outs,
        in_specs=[pl.BlockSpec(memory_space=pltpu.VMEM)] * len(operands),
        out_specs=specs,
        scratch_shapes=scratch,
        compiler_params=pltpu.CompilerParams(vmem_limit_bytes=40 * 2**20),
        cost_estimate=pl.CostEstimate(
            flops=flops, bytes_accessed=sum(o.size * o.dtype.itemsize for o in operands),
            transcendentals=0,
        ),
        name=name,
    )(*operands)


def grad(got, firsts, seconds, weight_in):
    width, hidden = weight_in.shape
    count, late = len(got), len(firsts)
    (before,) = local_call(
        functools.partial(part_kernel, count),
        "grad_part",
        (*got, weight_in),
        (pltpu.VMEM((hidden, width), jnp.float32),),
        flops=4 * CAP * count * width * hidden,
    )
    active, tail = local_call(
        functools.partial(active_kernel, late),
        "active_late",
        (*firsts, weight_in),
        (
            pltpu.VMEM((late * CAP, hidden), jnp.bfloat16),
            pltpu.VMEM((late, width), jnp.bfloat16),
        ),
        flops=2 * CAP * late * width * hidden,
    )
    (total,) = local_call(
        functools.partial(sum_kernel, late),
        "grad_sum",
        (*seconds, active, tail, before),
        (jax.ShapeDtypeStruct((hidden, width), jnp.bfloat16),),
        scratch=[pltpu.VMEM((hidden, width), jnp.bfloat16), pltpu.SemaphoreType.DMA((SEGS,))],
        flops=2 * CAP * late * width * hidden,
    )
    return total


def gather_both(down, up, n_pipe, cycle, cut):
    n = len(cycle)
    right = [(cycle[i], cycle[(i + 1) % n]) for i in range(n)]
    left = [(b, a) for a, b in right]

    def mirrored(block, moves):
        pairs = [(p * n + a, (n_pipe - 1 - p) * n + b) for p in range(n_pipe) for a, b in moves]
        return lax.ppermute(block, ("pipe", "expert"), pairs)

    def turn(at):
        up_left, down_right, up_right, down_left = at
        return (
            lax.ppermute(up_left, "expert", left),
            lax.ppermute(down_right, "expert", right),
            lax.ppermute(up_right, "expert", right),
            lax.ppermute(down_left, "expert", left),
        )

    at = (
        mirrored(up, left),
        lax.ppermute(down, "expert", right),
        mirrored(up, right),
        lax.ppermute(down, "expert", left),
    )
    got = [*at]
    for _ in range(1, (n - 1) // 2):
        at = turn(at)
        got += at
    firsts, seconds = (
        (lax.ppermute(l, "expert", left), lax.ppermute(r, "expert", right))
        for l, r in ((at[0][:, :cut], at[1][:, :cut]), (at[0][:, cut:], at[1][:, cut:]))
    )
    own = mirrored(up, [(e, e) for e in range(n)])
    return [*reversed(got), own, down], firsts, seconds


def body(
    tokens_down,
    cotan_down,
    gates_down,
    experts_down,
    tokens_up,
    cotan_up,
    gates_up,
    experts_up,
    w_in,
):
    n_pipe, n_expert = lax.axis_size("pipe"), lax.axis_size("expert")
    down, up = pack(
        (
            *(tokens_down[0], cotan_down[0], gates_down[0].T, experts_down[0].T),
            *(tokens_up[0], cotan_up[0], gates_up[0].T, experts_up[0].T),
        )
    )
    width = w_in.shape[1]
    cut = width + width // SEGS
    gathered = gather_both(down, up, n_pipe, grid_cycle(n_expert), cut)
    return grad(*gathered, w_in[0])[None]


def solution(mesh):
    rows = P("pipe", "expert", None)
    in_specs = (rows,) * 8 + (P("pipe", None, "expert"),)
    return jax.shard_map(body, mesh=mesh, in_specs=in_specs, out_specs=rows, check_vma=False)
```

```python
import functools

import jax
import jax.numpy as jnp
from jax import lax
from jax.experimental import pallas as pl
from jax.experimental.pallas import tpu as pltpu
from jax.sharding import PartitionSpec as P

CAP = 17
MAIN = 16
SEGS = 8
SHIFT = 2


def grid_cycle(n):
    fast = 1
    while 4 * fast * fast <= n:
        fast *= 2
    slow = n // fast
    order = [s * fast for s in range(slow)]
    for s in reversed(range(slow)):
        columns = range(1, fast)
        if (slow - 1 - s) % 2 == 1:
            columns = reversed(columns)
        order += [s * fast + c for c in columns]
    return order


def place(gates, ids):
    rows = ids.shape[1]
    named = ids == 0
    gate = jnp.sum(jnp.where(named, gates.astype(jnp.float32), 0.0), axis=0, keepdims=True)
    chosen = jnp.sum(named.astype(jnp.float32), axis=0, keepdims=True)
    earlier = (
        lax.broadcasted_iota(jnp.int32, (rows, rows), 0)
        < lax.broadcasted_iota(jnp.int32, (rows, rows), 1)
    ).astype(jnp.float32)
    slot = jnp.dot(
        jnp.broadcast_to(chosen, (8, rows)), earlier, preferred_element_type=jnp.float32
    )[:1].astype(jnp.int32)
    want = lax.broadcasted_iota(jnp.int32, (2 * MAIN, rows), 0)
    hit = (want == slot) & (chosen > 0.0) & (want < CAP)
    slot_gate = jnp.sum(jnp.where(hit, gate, 0.0), axis=1, keepdims=True)
    return hit.astype(jnp.bfloat16), slot_gate


def pack_kernel(*refs):
    hbm, outs, held, sems = refs[:8], refs[8:10], refs[10:18], refs[18]
    order = [2, 3, 6, 7, 4, 5, 0, 1]
    copies = {i: pltpu.make_async_copy(hbm[i], held[i], sems.at[i]) for i in order}
    for i in order:
        copies[i].start()
    for i in order[:4]:
        copies[i].wait()
    places = [place(held[d + 2][...], held[d + 3][...]) for d in (0, 4)]
    for d, (placing, slot_gate), out_ref in ((4, places[1], outs[1]), (0, places[0], outs[0])):
        copies[d].wait()
        copies[d + 1].wait()
        width = held[d].shape[1]
        seg = width // SEGS
        x = jnp.dot(placing, held[d][...], preferred_element_type=jnp.float32)
        y = jnp.dot(placing, held[d + 1][...], preferred_element_type=jnp.float32) * slot_gate
        out_ref[:, :width] = x[:MAIN].astype(jnp.bfloat16)
        out_ref[:, width + seg :] = y[:MAIN].astype(jnp.bfloat16)
        tail = [x[MAIN : MAIN + 1, s * seg : (s + 1) * seg] for s in range(SEGS)]
        tail += [y[MAIN : MAIN + 1, s * seg : (s + 1) * seg] for s in range(SEGS)]
        out_ref[:, width : width + seg] = jnp.concatenate(tail, axis=0).astype(jnp.bfloat16)


def pack(arrays):
    rows, width = arrays[0].shape
    seg = width // SEGS
    payload = pltpu.VMEM((MAIN, 2 * width + seg), jnp.bfloat16)
    arrays = [pltpu.with_memory_space_constraint(a, pltpu.HBM) for a in arrays]
    return pl.pallas_call(
        pack_kernel,
        out_shape=(payload, payload),
        in_specs=[pl.BlockSpec(memory_space=pltpu.HBM)] * 8,
        out_specs=(pl.BlockSpec(memory_space=pltpu.VMEM),) * 2,
        scratch_shapes=[pltpu.VMEM(a.shape, a.dtype) for a in arrays]
        + [pltpu.SemaphoreType.DMA((8,))],
        compiler_params=pltpu.CompilerParams(vmem_limit_bytes=16 * 2**20),
        cost_estimate=pl.CostEstimate(
            flops=8 * 2 * MAIN * rows * width, bytes_accessed=12 * rows * width, transcendentals=0
        ),
        name="pack_slots",
    )(*arrays)


def activate(payloads, w_ref):
    count, width = len(payloads), w_ref.shape[0]
    seg = width // SEGS
    size = count * 2 * SEGS
    tails = jnp.concatenate([p[:, width : width + seg] for p in payloads], axis=0)
    row = lax.broadcasted_iota(jnp.int32, (size, size), 0)
    col = lax.broadcasted_iota(jnp.int32, (size, size), 1)
    order = ((row % count) * (2 * SEGS) + row // count == col).astype(jnp.bfloat16)
    tails = jnp.dot(order, tails, preferred_element_type=jnp.float32)
    x_tail, y_tail = (
        jnp.concatenate(
            [tails[s * count : (s + 1) * count] for s in range(first, first + SEGS)], axis=1
        ).astype(jnp.bfloat16)
        for first in (0, SEGS)
    )
    rows_x = jnp.concatenate([p[:, :width] for p in payloads] + [x_tail], axis=0)
    hidden = jnp.dot(rows_x, w_ref[...], preferred_element_type=jnp.float32)
    return (hidden * jax.nn.sigmoid(hidden)).astype(jnp.bfloat16), y_tail


def times(active, rows_y):
    return lax.dot_general(
        active, rows_y, (((0,), (0,)), ((), ())), preferred_element_type=jnp.float32
    )


def part_kernel(count, *refs):
    payloads, (w_ref, out_ref) = refs[:count], refs[count:]
    width = w_ref.shape[0]
    seg = width // SEGS
    active, y_tail = activate(payloads, w_ref)
    for s in range(SEGS):
        here = slice(s * seg, (s + 1) * seg)
        there = slice(width + (s + 1) * seg, width + (s + 2) * seg)
        rows_y = jnp.concatenate([p[:, there] for p in payloads] + [y_tail[:, here]], axis=0)
        out_ref[:, here] = times(active, rows_y)


def active_kernel(count, *refs):
    payloads, (w_ref, active_ref, tail_ref) = refs[:count], refs[count:]
    active_ref[...], tail_ref[...] = activate(payloads, w_ref)


def sum_kernel(count, starts, *refs):
    pieces, (active_ref, tail_ref, before, out_ref, made, sems) = refs[:count], refs[count:]
    width = tail_ref.shape[1]
    seg = width // SEGS
    active = active_ref[...]
    copies = []
    for s in range(SEGS):
        here = slice(s * seg, (s + 1) * seg)
        rows_y = []
        for ends in starts:
            index, first, lanes = [e for e in ends if e[1] <= here.start][-1]
            at = lanes + here.start - first
            rows_y.append(pieces[index][:, at : at + seg])
        rows_y = jnp.concatenate(rows_y + [tail_ref[:, here]], axis=0)
        made[:, here] = (before[:, here] + times(active, rows_y)).astype(jnp.bfloat16)
        copies.append(
            pltpu.make_async_copy(made.at[:, here], out_ref.at[:, here], sems.at[s])
        )
        copies[-1].start()
    for copy in copies:
        copy.wait()


def local_call(kernel, name, operands, outs, scratch=(), flops=0):
    specs = tuple(
        pl.BlockSpec(
            memory_space=pltpu.HBM if isinstance(out, jax.ShapeDtypeStruct) else pltpu.VMEM
        )
        for out in outs
    )
    return pl.pallas_call(
        kernel,
        out_shape=outs,
        in_specs=[pl.BlockSpec(memory_space=pltpu.VMEM)] * len(operands),
        out_specs=specs,
        scratch_shapes=scratch,
        compiler_params=pltpu.CompilerParams(vmem_limit_bytes=40 * 2**20),
        cost_estimate=pl.CostEstimate(
            flops=flops, bytes_accessed=sum(o.size * o.dtype.itemsize for o in operands),
            transcendentals=0,
        ),
        name=name,
    )(*operands)


def grad_part(blocks, weight_in):
    width, hidden = weight_in.shape
    (part,) = local_call(
        functools.partial(part_kernel, len(blocks)),
        "grad_part",
        (*blocks, weight_in),
        (pltpu.VMEM((hidden, width), jnp.float32),),
        flops=4 * CAP * len(blocks) * width * hidden,
    )
    return part


def grad_sum(late, pieces, starts, weight_in, before):
    width, hidden = weight_in.shape
    count = len(late)
    active, tail = local_call(
        functools.partial(active_kernel, count),
        "active_late",
        (*late, weight_in),
        (
            pltpu.VMEM((count * CAP, hidden), jnp.bfloat16),
            pltpu.VMEM((count, width), jnp.bfloat16),
        ),
        flops=2 * CAP * count * width * hidden,
    )
    (total,) = local_call(
        functools.partial(sum_kernel, len(pieces), starts),
        "grad_sum",
        (*pieces, active, tail, before),
        (jax.ShapeDtypeStruct((hidden, width), jnp.bfloat16),),
        scratch=[pltpu.VMEM((hidden, width), jnp.bfloat16), pltpu.SemaphoreType.DMA((SEGS,))],
        flops=2 * CAP * count * width * hidden,
    )
    return total


def gather_and_multiply(down, up, weight_in, n_pipe, cycle):
    n = len(cycle)
    right = [(cycle[i], cycle[(i + 1) % n]) for i in range(n)]
    left = [(b, a) for a, b in right]

    def mirrored(block, moves):
        pairs = [(p * n + a, (n_pipe - 1 - p) * n + b) for p in range(n_pipe) for a, b in moves]
        return lax.ppermute(block, ("pipe", "expert"), pairs)

    def turn(at):
        up_left, down_right, up_right, down_left = at
        return (
            lax.ppermute(up_left, "expert", left),
            lax.ppermute(down_right, "expert", right),
            lax.ppermute(up_right, "expert", right),
            lax.ppermute(down_left, "expert", left),
        )

    at = (
        mirrored(up, left),
        lax.ppermute(down, "expert", right),
        mirrored(up, right),
        lax.ppermute(down, "expert", left),
    )
    early = [*at]
    for _ in range(2, (n - 1) // 2):
        at = turn(at)
        early += at
    own = mirrored(up, [(e, e) for e in range(n)])
    part = grad_part([*reversed(early), own, down], weight_in)
    at = turn(at)
    at0, _ = lax.optimization_barrier((at[0], part))
    at = (at0, *at[1:])
    up_left, down_right, up_right, down_left = at
    width = weight_in.shape[0]
    cut = width + width // SEGS
    up_last = lax.ppermute(up_left, "expert", left)
    down_first = lax.ppermute(down_right[:, :cut], "expert", right)
    shift = width - SHIFT * (width // SEGS)
    late = (down_left, up_right, down_right, up_left, up_last, down_first)
    pieces = (
        *late[:-1],
        lax.ppermute(down_left[:, cut + shift :], "expert", left),
        lax.ppermute(down_right[:, cut : cut + shift], "expert", right),
    )
    last = len(late) - 1
    starts = [((i, 0, cut),) for i in range(last)]
    starts += [((last + 1, 0, 0), (last, shift, 0))]
    return grad_sum(late, pieces, starts, weight_in, part)


def body(
    tokens_down,
    cotan_down,
    gates_down,
    experts_down,
    tokens_up,
    cotan_up,
    gates_up,
    experts_up,
    w_in,
):
    n_pipe, n_expert = lax.axis_size("pipe"), lax.axis_size("expert")
    down, up = pack(
        (
            *(tokens_down[0], cotan_down[0], gates_down[0].T, experts_down[0].T),
            *(tokens_up[0], cotan_up[0], gates_up[0].T, experts_up[0].T),
        )
    )
    return gather_and_multiply(down, up, w_in[0], n_pipe, grid_cycle(n_expert))[None]


def solution(mesh):
    rows = P("pipe", "expert", None)
    in_specs = (rows,) * 8 + (P("pipe", None, "expert"),)
    return jax.shard_map(body, mesh=mesh, in_specs=in_specs, out_specs=rows, check_vma=False)
```

```python
import functools

import jax
import jax.numpy as jnp
from jax import lax
from jax.experimental import pallas as pl
from jax.experimental.pallas import tpu as pltpu
from jax.sharding import PartitionSpec as P

CAP = 17
MAIN = 16
SEGS = 8


def grid_cycle(n):
    fast = 1
    while 4 * fast * fast <= n:
        fast *= 2
    slow = n // fast
    order = [s * fast for s in range(slow)]
    for s in reversed(range(slow)):
        columns = range(1, fast)
        if (slow - 1 - s) % 2 == 1:
            columns = reversed(columns)
        order += [s * fast + c for c in columns]
    return order


def place(gates, ids):
    rows = ids.shape[1]
    named = ids == 0
    gate = jnp.sum(jnp.where(named, gates.astype(jnp.float32), 0.0), axis=0, keepdims=True)
    chosen = jnp.sum(named.astype(jnp.float32), axis=0, keepdims=True)
    earlier = (
        lax.broadcasted_iota(jnp.int32, (rows, rows), 0)
        < lax.broadcasted_iota(jnp.int32, (rows, rows), 1)
    ).astype(jnp.float32)
    slot = jnp.dot(
        jnp.broadcast_to(chosen, (8, rows)), earlier, preferred_element_type=jnp.float32
    )[:1].astype(jnp.int32)
    want = lax.broadcasted_iota(jnp.int32, (2 * MAIN, rows), 0)
    hit = (want == slot) & (chosen > 0.0) & (want < CAP)
    slot_gate = jnp.sum(jnp.where(hit, gate, 0.0), axis=1, keepdims=True)
    return hit.astype(jnp.bfloat16), slot_gate


def pack_kernel(*refs):
    hbm, outs, held, sems = refs[:8], refs[8:10], refs[10:18], refs[18]
    order = [2, 3, 6, 7, 4, 5, 0, 1]
    copies = {i: pltpu.make_async_copy(hbm[i], held[i], sems.at[i]) for i in order}
    for i in order:
        copies[i].start()
    for i in order[:4]:
        copies[i].wait()
    places = [place(held[d + 2][...], held[d + 3][...]) for d in (0, 4)]
    for d, (placing, slot_gate), out_ref in ((4, places[1], outs[1]), (0, places[0], outs[0])):
        copies[d].wait()
        copies[d + 1].wait()
        width = held[d].shape[1]
        seg = width // SEGS
        x = jnp.dot(placing, held[d][...], preferred_element_type=jnp.float32)
        y = jnp.dot(placing, held[d + 1][...], preferred_element_type=jnp.float32) * slot_gate
        out_ref[:, :width] = x[:MAIN].astype(jnp.bfloat16)
        out_ref[:, width + seg :] = y[:MAIN].astype(jnp.bfloat16)
        tail = [x[MAIN : MAIN + 1, s * seg : (s + 1) * seg] for s in range(SEGS)]
        tail += [y[MAIN : MAIN + 1, s * seg : (s + 1) * seg] for s in range(SEGS)]
        out_ref[:, width : width + seg] = jnp.concatenate(tail, axis=0).astype(jnp.bfloat16)


def pack(arrays):
    rows, width = arrays[0].shape
    seg = width // SEGS
    payload = pltpu.VMEM((MAIN, 2 * width + seg), jnp.bfloat16)
    arrays = [pltpu.with_memory_space_constraint(a, pltpu.HBM) for a in arrays]
    return pl.pallas_call(
        pack_kernel,
        out_shape=(payload, payload),
        in_specs=[pl.BlockSpec(memory_space=pltpu.HBM)] * 8,
        out_specs=(pl.BlockSpec(memory_space=pltpu.VMEM),) * 2,
        scratch_shapes=[pltpu.VMEM(a.shape, a.dtype) for a in arrays]
        + [pltpu.SemaphoreType.DMA((8,))],
        compiler_params=pltpu.CompilerParams(vmem_limit_bytes=16 * 2**20),
        cost_estimate=pl.CostEstimate(
            flops=8 * 2 * MAIN * rows * width, bytes_accessed=12 * rows * width, transcendentals=0
        ),
        name="pack_slots",
    )(*arrays)


def activate(payloads, w_ref):
    count, width = len(payloads), w_ref.shape[0]
    seg = width // SEGS
    size = count * 2 * SEGS
    tails = jnp.concatenate([p[:, width : width + seg] for p in payloads], axis=0)
    row = lax.broadcasted_iota(jnp.int32, (size, size), 0)
    col = lax.broadcasted_iota(jnp.int32, (size, size), 1)
    order = ((row % count) * (2 * SEGS) + row // count == col).astype(jnp.bfloat16)
    tails = jnp.dot(order, tails, preferred_element_type=jnp.float32)
    x_tail, y_tail = (
        jnp.concatenate(
            [tails[s * count : (s + 1) * count] for s in range(first, first + SEGS)], axis=1
        ).astype(jnp.bfloat16)
        for first in (0, SEGS)
    )
    rows_x = jnp.concatenate([p[:, :width] for p in payloads] + [x_tail], axis=0)
    hidden = jnp.dot(rows_x, w_ref[...], preferred_element_type=jnp.float32)
    return (hidden * jax.nn.sigmoid(hidden)).astype(jnp.bfloat16), y_tail


def times(active, rows_y):
    return lax.dot_general(
        active, rows_y, (((0,), (0,)), ((), ())), preferred_element_type=jnp.float32
    )


def part_kernel(count, *refs):
    payloads, (w_ref, out_ref) = refs[:count], refs[count:]
    width = w_ref.shape[0]
    seg = width // SEGS
    active, y_tail = activate(payloads, w_ref)
    for s in range(SEGS):
        here = slice(s * seg, (s + 1) * seg)
        there = slice(width + (s + 1) * seg, width + (s + 2) * seg)
        rows_y = jnp.concatenate([p[:, there] for p in payloads] + [y_tail[:, here]], axis=0)
        out_ref[:, here] = times(active, rows_y)


def active_kernel(count, *refs):
    payloads, (w_ref, active_ref, tail_ref) = refs[:count], refs[count:]
    active_ref[...], tail_ref[...] = activate(payloads, w_ref)


def sum_kernel(count, *refs):
    blocks, (active_ref, tail_ref, before, out_ref, made, sems) = refs[:count], refs[count:]
    seg = tail_ref.shape[1] // SEGS
    active = active_ref[...]
    copies = []
    for s in range(SEGS):
        here = slice(s * seg, (s + 1) * seg)
        rows_y = jnp.concatenate([b[:, here] for b in blocks] + [tail_ref[:, here]], axis=0)
        made[:, here] = (before[:, here] + times(active, rows_y)).astype(jnp.bfloat16)
        copies.append(
            pltpu.make_async_copy(made.at[:, here], out_ref.at[:, here], sems.at[s])
        )
        copies[-1].start()
    for copy in copies:
        copy.wait()


def local_call(kernel, name, operands, outs, scratch=(), flops=0):
    specs = tuple(
        pl.BlockSpec(
            memory_space=pltpu.HBM if isinstance(out, jax.ShapeDtypeStruct) else pltpu.VMEM
        )
        for out in outs
    )
    return pl.pallas_call(
        kernel,
        out_shape=outs,
        in_specs=[pl.BlockSpec(memory_space=pltpu.VMEM)] * len(operands),
        out_specs=specs,
        scratch_shapes=scratch,
        compiler_params=pltpu.CompilerParams(vmem_limit_bytes=40 * 2**20),
        cost_estimate=pl.CostEstimate(
            flops=flops, bytes_accessed=sum(o.size * o.dtype.itemsize for o in operands),
            transcendentals=0,
        ),
        name=name,
    )(*operands)


def grad(got, firsts, seconds, weight_in):
    width, hidden = weight_in.shape
    count, late = len(got), len(firsts)
    (before,) = local_call(
        functools.partial(part_kernel, count),
        "grad_part",
        (*got, weight_in),
        (pltpu.VMEM((hidden, width), jnp.float32),),
        flops=4 * CAP * count * width * hidden,
    )
    active, tail = local_call(
        functools.partial(active_kernel, late),
        "active_late",
        (*firsts, weight_in),
        (
            pltpu.VMEM((late * CAP, hidden), jnp.bfloat16),
            pltpu.VMEM((late, width), jnp.bfloat16),
        ),
        flops=2 * CAP * late * width * hidden,
    )
    (total,) = local_call(
        functools.partial(sum_kernel, late),
        "grad_sum",
        (*seconds, active, tail, before),
        (jax.ShapeDtypeStruct((hidden, width), jnp.bfloat16),),
        scratch=[pltpu.VMEM((hidden, width), jnp.bfloat16), pltpu.SemaphoreType.DMA((SEGS,))],
        flops=2 * CAP * late * width * hidden,
    )
    return total


def gather_both(down, up, n_pipe, cycle, cut):
    n = len(cycle)
    right = [(cycle[i], cycle[(i + 1) % n]) for i in range(n)]
    left = [(b, a) for a, b in right]

    def move(block, moves, mirrored=False):
        pairs = []
        for p in range(n_pipe):
            turned = p % 2 != 2 * p // n_pipe
            to = n_pipe - 1 - p if mirrored else p
            pairs += [(p * n + (b if turned else a), to * n + (a if turned else b)) for a, b in moves]
        return lax.ppermute(block, ("pipe", "expert"), pairs)

    def turn(at):
        up_left, down_right, up_right, down_left = at
        return (
            move(up_left, left),
            move(down_right, right),
            move(up_right, right),
            move(down_left, left),
        )

    at = (
        move(up, left, mirrored=True),
        move(down, right),
        move(up, right, mirrored=True),
        move(down, left),
    )
    got = [*at]
    for _ in range(1, (n - 1) // 2):
        at = turn(at)
        got += at
    firsts, seconds = (
        (move(l, left), move(r, right))
        for l, r in ((at[0][:, :cut], at[1][:, :cut]), (at[0][:, cut:], at[1][:, cut:]))
    )
    own = move(up, [(e, e) for e in range(n)], mirrored=True)
    return [*reversed(got), own, down], firsts, seconds


def body(
    tokens_down,
    cotan_down,
    gates_down,
    experts_down,
    tokens_up,
    cotan_up,
    gates_up,
    experts_up,
    w_in,
):
    n_pipe, n_expert = lax.axis_size("pipe"), lax.axis_size("expert")
    down, up = pack(
        (
            *(tokens_down[0], cotan_down[0], gates_down[0].T, experts_down[0].T),
            *(tokens_up[0], cotan_up[0], gates_up[0].T, experts_up[0].T),
        )
    )
    width = w_in.shape[1]
    cut = width + width // SEGS
    gathered = gather_both(down, up, n_pipe, grid_cycle(n_expert), cut)
    return grad(*gathered, w_in[0])[None]


def solution(mesh):
    rows = P("pipe", "expert", None)
    in_specs = (rows,) * 8 + (P("pipe", None, "expert"),)
    return jax.shard_map(body, mesh=mesh, in_specs=in_specs, out_specs=rows, check_vma=False)
```

```python
import functools

import jax
import jax.numpy as jnp
from jax import lax
from jax.experimental import pallas as pl
from jax.experimental.pallas import tpu as pltpu
from jax.sharding import PartitionSpec as P

CAP = 17
MAIN = 16
SEGS = 8


def grid_cycle(n):
    fast = 1
    while 4 * fast * fast <= n:
        fast *= 2
    slow = n // fast
    order = [s * fast for s in range(slow)]
    for s in reversed(range(slow)):
        columns = range(1, fast)
        if (slow - 1 - s) % 2 == 1:
            columns = reversed(columns)
        order += [s * fast + c for c in columns]
    return order


def place(gates, ids):
    rows = ids.shape[1]
    named = ids == 0
    gate = jnp.sum(jnp.where(named, gates.astype(jnp.float32), 0.0), axis=0, keepdims=True)
    chosen = jnp.sum(named.astype(jnp.float32), axis=0, keepdims=True)
    earlier = (
        lax.broadcasted_iota(jnp.int32, (rows, rows), 0)
        < lax.broadcasted_iota(jnp.int32, (rows, rows), 1)
    ).astype(jnp.float32)
    slot = jnp.dot(
        jnp.broadcast_to(chosen, (8, rows)), earlier, preferred_element_type=jnp.float32
    )[:1].astype(jnp.int32)
    want = lax.broadcasted_iota(jnp.int32, (2 * MAIN, rows), 0)
    hit = (want == slot) & (chosen > 0.0) & (want < CAP)
    slot_gate = jnp.sum(jnp.where(hit, gate, 0.0), axis=1, keepdims=True)
    return hit.astype(jnp.bfloat16), slot_gate


def is_turned(p, n_pipe):
    return p % 2 != 2 * p // n_pipe


def pack_kernel(n_pipe, *refs):
    hbm, (lead, trail, up, down), held, sems = refs[:8], refs[8:12], refs[12:20], refs[20]
    order = (2, 3, 6, 7, 0, 1, 4, 5)
    turned = is_turned(lax.axis_index("pipe"), n_pipe)

    def copies(swapped):
        sources = hbm[:4] + hbm[4:] if swapped else hbm[4:] + hbm[:4]
        return [pltpu.make_async_copy(sources[i], held[i], sems.at[i]) for i in order]

    for swapped in (False, True):

        @pl.when(turned == swapped)
        def _():
            for copy in copies(swapped):
                copy.start()

    waits = dict(zip(order, copies(False)))
    for i in order[:4]:
        waits[i].wait()
    places = [place(held[d + 2][...], held[d + 3][...]) for d in (0, 4)]
    for d, (placing, slot_gate), out_ref in ((0, places[0], lead), (4, places[1], trail)):
        waits[d].wait()
        waits[d + 1].wait()
        width = held[d].shape[1]
        seg = width // SEGS
        x = jnp.dot(placing, held[d][...], preferred_element_type=jnp.float32)
        y = jnp.dot(placing, held[d + 1][...], preferred_element_type=jnp.float32) * slot_gate
        out_ref[:, :width] = x[:MAIN].astype(jnp.bfloat16)
        out_ref[:, width + seg :] = y[:MAIN].astype(jnp.bfloat16)
        tail = [x[MAIN : MAIN + 1, s * seg : (s + 1) * seg] for s in range(SEGS)]
        tail += [y[MAIN : MAIN + 1, s * seg : (s + 1) * seg] for s in range(SEGS)]
        out_ref[:, width : width + seg] = jnp.concatenate(tail, axis=0).astype(jnp.bfloat16)
    for swapped, first, second in ((False, up, down), (True, down, up)):

        @pl.when(turned == swapped)
        def _():
            first[...] = lead[...]
            second[...] = trail[...]


def pack(arrays, n_pipe):
    rows, width = arrays[0].shape
    seg = width // SEGS
    payload = pltpu.VMEM((MAIN, 2 * width + seg), jnp.bfloat16)
    arrays = [pltpu.with_memory_space_constraint(a, pltpu.HBM) for a in arrays]
    return pl.pallas_call(
        functools.partial(pack_kernel, n_pipe),
        out_shape=(payload,) * 4,
        in_specs=[pl.BlockSpec(memory_space=pltpu.HBM)] * 8,
        out_specs=(pl.BlockSpec(memory_space=pltpu.VMEM),) * 4,
        scratch_shapes=[pltpu.VMEM(a.shape, a.dtype) for a in arrays]
        + [pltpu.SemaphoreType.DMA((8,))],
        compiler_params=pltpu.CompilerParams(vmem_limit_bytes=16 * 2**20),
        cost_estimate=pl.CostEstimate(
            flops=8 * 2 * MAIN * rows * width, bytes_accessed=12 * rows * width, transcendentals=0
        ),
        name="pack_slots",
    )(*arrays)


def activate(payloads, w_ref):
    count, width = len(payloads), w_ref.shape[0]
    seg = width // SEGS
    size = count * 2 * SEGS
    tails = jnp.concatenate([p[:, width : width + seg] for p in payloads], axis=0)
    row = lax.broadcasted_iota(jnp.int32, (size, size), 0)
    col = lax.broadcasted_iota(jnp.int32, (size, size), 1)
    order = ((row % count) * (2 * SEGS) + row // count == col).astype(jnp.bfloat16)
    tails = jnp.dot(order, tails, preferred_element_type=jnp.float32)
    x_tail, y_tail = (
        jnp.concatenate(
            [tails[s * count : (s + 1) * count] for s in range(first, first + SEGS)], axis=1
        ).astype(jnp.bfloat16)
        for first in (0, SEGS)
    )
    rows_x = jnp.concatenate([p[:, :width] for p in payloads] + [x_tail], axis=0)
    hidden = jnp.dot(rows_x, w_ref[...], preferred_element_type=jnp.float32)
    return (hidden * jax.nn.sigmoid(hidden)).astype(jnp.bfloat16), y_tail


def times(active, rows_y):
    return lax.dot_general(
        active, rows_y, (((0,), (0,)), ((), ())), preferred_element_type=jnp.float32
    )


def part_kernel(count, *refs):
    payloads, (w_ref, out_ref) = refs[:count], refs[count:]
    width = w_ref.shape[0]
    seg = width // SEGS
    active, y_tail = activate(payloads, w_ref)
    for s in range(SEGS):
        here = slice(s * seg, (s + 1) * seg)
        there = slice(width + (s + 1) * seg, width + (s + 2) * seg)
        rows_y = jnp.concatenate([p[:, there] for p in payloads] + [y_tail[:, here]], axis=0)
        out_ref[:, here] = times(active, rows_y)


def active_kernel(count, *refs):
    payloads, (w_ref, active_ref, tail_ref) = refs[:count], refs[count:]
    active_ref[...], tail_ref[...] = activate(payloads, w_ref)


def sum_kernel(count, *refs):
    blocks, (active_ref, tail_ref, before, out_ref, made, sems) = refs[:count], refs[count:]
    seg = tail_ref.shape[1] // SEGS
    active = active_ref[...]
    copies = []
    for s in range(SEGS):
        here = slice(s * seg, (s + 1) * seg)
        rows_y = jnp.concatenate([b[:, here] for b in blocks] + [tail_ref[:, here]], axis=0)
        made[:, here] = (before[:, here] + times(active, rows_y)).astype(jnp.bfloat16)
        copies.append(
            pltpu.make_async_copy(made.at[:, here], out_ref.at[:, here], sems.at[0])
        )
        copies[-1].start()
    pltpu.make_async_copy(made, out_ref, sems.at[0]).wait()


def local_call(kernel, name, operands, outs, scratch=(), flops=0):
    specs = tuple(
        pl.BlockSpec(
            memory_space=pltpu.HBM if isinstance(out, jax.ShapeDtypeStruct) else pltpu.VMEM
        )
        for out in outs
    )
    return pl.pallas_call(
        kernel,
        out_shape=outs,
        in_specs=[pl.BlockSpec(memory_space=pltpu.VMEM)] * len(operands),
        out_specs=specs,
        scratch_shapes=scratch,
        compiler_params=pltpu.CompilerParams(vmem_limit_bytes=40 * 2**20),
        cost_estimate=pl.CostEstimate(
            flops=flops, bytes_accessed=sum(o.size * o.dtype.itemsize for o in operands),
            transcendentals=0,
        ),
        name=name,
    )(*operands)


def grad(got, firsts, seconds, weight_in):
    width, hidden = weight_in.shape
    count, late = len(got), len(firsts)
    (before,) = local_call(
        functools.partial(part_kernel, count),
        "grad_part",
        (*got, weight_in),
        (pltpu.VMEM((hidden, width), jnp.float32),),
        flops=4 * CAP * count * width * hidden,
    )
    active, tail = local_call(
        functools.partial(active_kernel, late),
        "active_late",
        (*firsts, weight_in),
        (
            pltpu.VMEM((late * CAP, hidden), jnp.bfloat16),
            pltpu.VMEM((late, width), jnp.bfloat16),
        ),
        flops=2 * CAP * late * width * hidden,
    )
    (total,) = local_call(
        functools.partial(sum_kernel, late),
        "grad_sum",
        (*seconds, active, tail, before),
        (jax.ShapeDtypeStruct((hidden, width), jnp.bfloat16),),
        scratch=[pltpu.VMEM((hidden, width), jnp.bfloat16), pltpu.SemaphoreType.DMA((SEGS,))],
        flops=2 * CAP * late * width * hidden,
    )
    return total


def gather_both(lead, trail, up, n_pipe, cycle, cut):
    n = len(cycle)
    right = [(cycle[i], cycle[(i + 1) % n]) for i in range(n)]
    left = [(b, a) for a, b in right]

    def move(block, moves, mirrored=lambda turned: False):
        pairs = []
        for p in range(n_pipe):
            turned = is_turned(p, n_pipe)
            to = n_pipe - 1 - p if mirrored(turned) else p
            pairs += [(p * n + (b if turned else a), to * n + (a if turned else b)) for a, b in moves]
        return lax.ppermute(block, ("pipe", "expert"), pairs)

    def turn(at):
        return (move(at[0], left), move(at[1], right), move(at[2], right), move(at[3], left))

    at = (
        move(lead, left, lambda turned: not turned),
        move(trail, right, lambda turned: turned),
        move(lead, right, lambda turned: not turned),
        move(trail, left, lambda turned: turned),
    )
    got = [*at]
    for _ in range(1, (n - 1) // 2):
        at = turn(at)
        got += at
    firsts, seconds = (
        (move(l, left), move(r, right))
        for l, r in ((at[0][:, :cut], at[1][:, :cut]), (at[0][:, cut:], at[1][:, cut:]))
    )
    own = move(up, [(e, e) for e in range(n)], lambda turned: True)
    return [*reversed(got), own], firsts, seconds


def body(
    tokens_down,
    cotan_down,
    gates_down,
    experts_down,
    tokens_up,
    cotan_up,
    gates_up,
    experts_up,
    w_in,
):
    n_pipe, n_expert = lax.axis_size("pipe"), lax.axis_size("expert")
    lead, trail, up, down = pack(
        (
            *(tokens_down[0], cotan_down[0], gates_down[0].T, experts_down[0].T),
            *(tokens_up[0], cotan_up[0], gates_up[0].T, experts_up[0].T),
        ),
        n_pipe,
    )
    width = w_in.shape[1]
    cut = width + width // SEGS
    got, firsts, seconds = gather_both(lead, trail, up, n_pipe, grid_cycle(n_expert), cut)
    return grad([*got, down], firsts, seconds, w_in[0])[None]


def solution(mesh):
    rows = P("pipe", "expert", None)
    in_specs = (rows,) * 8 + (P("pipe", None, "expert"),)
    return jax.shard_map(body, mesh=mesh, in_specs=in_specs, out_specs=rows, check_vma=False)
```

```python
import functools

import jax
import jax.numpy as jnp
from jax import lax
from jax.experimental import pallas as pl
from jax.experimental.pallas import tpu as pltpu
from jax.sharding import PartitionSpec as P

CAP = 17
MAIN = 16
SEGS = 8


def grid_cycle(n):
    fast = 1
    while 4 * fast * fast <= n:
        fast *= 2
    slow = n // fast
    order = [s * fast for s in range(slow)]
    for s in reversed(range(slow)):
        columns = range(1, fast)
        if (slow - 1 - s) % 2 == 1:
            columns = reversed(columns)
        order += [s * fast + c for c in columns]
    return order


def place(gates, ids):
    rows = ids.shape[1]
    named = ids == 0
    gate = jnp.sum(jnp.where(named, gates.astype(jnp.float32), 0.0), axis=0, keepdims=True)
    chosen = jnp.sum(named.astype(jnp.float32), axis=0, keepdims=True)
    earlier = (
        lax.broadcasted_iota(jnp.int32, (rows, rows), 0)
        < lax.broadcasted_iota(jnp.int32, (rows, rows), 1)
    ).astype(jnp.float32)
    slot = jnp.dot(
        jnp.broadcast_to(chosen, (8, rows)), earlier, preferred_element_type=jnp.float32
    )[:1].astype(jnp.int32)
    want = lax.broadcasted_iota(jnp.int32, (2 * MAIN, rows), 0)
    hit = (want == slot) & (chosen > 0.0) & (want < CAP)
    slot_gate = jnp.sum(jnp.where(hit, gate, 0.0), axis=1, keepdims=True)
    return hit.astype(jnp.bfloat16), slot_gate


def is_turned(p, n_pipe):
    return p % 2 != 2 * p // n_pipe


def write_payload(out_ref, tokens_ref, cotan_ref, placing, slot_gate):
    width = tokens_ref.shape[1]
    seg = width // SEGS
    x = jnp.dot(placing, tokens_ref[...], preferred_element_type=jnp.float32)
    y = jnp.dot(placing, cotan_ref[...], preferred_element_type=jnp.float32) * slot_gate
    out_ref[:, :width] = x[:MAIN].astype(jnp.bfloat16)
    out_ref[:, width + seg :] = y[:MAIN].astype(jnp.bfloat16)
    tail = [x[MAIN : MAIN + 1, s * seg : (s + 1) * seg] for s in range(SEGS)]
    tail += [y[MAIN : MAIN + 1, s * seg : (s + 1) * seg] for s in range(SEGS)]
    out_ref[:, width : width + seg] = jnp.concatenate(tail, axis=0).astype(jnp.bfloat16)


def lead_kernel(n_pipe, *refs):
    hbm, lead, trail, (tokens_ref, cotan_ref, gates_ref, ids_ref, sems) = (
        refs[:8],
        refs[8],
        refs[9:13],
        refs[13:],
    )
    held = (tokens_ref, cotan_ref, gates_ref, ids_ref, *trail)
    order = (2, 3, 0, 1, 6, 7, 4, 5)
    turned = is_turned(lax.axis_index("pipe"), n_pipe)

    def copies(swapped):
        sources = hbm[:4] + hbm[4:] if swapped else hbm[4:] + hbm[:4]
        return {i: pltpu.make_async_copy(sources[i], held[i], sems.at[i]) for i in order}

    for swapped in (False, True):

        @pl.when(turned == swapped)
        def _():
            for copy in copies(swapped).values():
                copy.start()

    waits = copies(False)
    waits[2].wait()
    waits[3].wait()
    placed = place(gates_ref[...], ids_ref[...])
    waits[0].wait()
    waits[1].wait()
    write_payload(lead, tokens_ref, cotan_ref, *placed)
    for i in range(4, 8):
        waits[i].wait()


def trail_kernel(n_pipe, lead, tokens_ref, cotan_ref, gates_ref, ids_ref, trail, up, down):
    write_payload(trail, tokens_ref, cotan_ref, *place(gates_ref[...], ids_ref[...]))
    turned = is_turned(lax.axis_index("pipe"), n_pipe)
    for swapped, first, second in ((False, up, down), (True, down, up)):

        @pl.when(turned == swapped)
        def _():
            first[...] = lead[...]
            second[...] = trail[...]


def pack(arrays, n_pipe):
    rows, width = arrays[0].shape
    seg = width // SEGS
    payload = pltpu.VMEM((MAIN, 2 * width + seg), jnp.bfloat16)
    arrays = [pltpu.with_memory_space_constraint(a, pltpu.HBM) for a in arrays]
    lead, *trail = pl.pallas_call(
        functools.partial(lead_kernel, n_pipe),
        out_shape=(payload, *(pltpu.VMEM(a.shape, a.dtype) for a in arrays[:4])),
        in_specs=[pl.BlockSpec(memory_space=pltpu.HBM)] * 8,
        out_specs=(pl.BlockSpec(memory_space=pltpu.VMEM),) * 5,
        scratch_shapes=[pltpu.VMEM(a.shape, a.dtype) for a in arrays[:4]]
        + [pltpu.SemaphoreType.DMA((8,))],
        compiler_params=pltpu.CompilerParams(vmem_limit_bytes=16 * 2**20),
        cost_estimate=pl.CostEstimate(
            flops=4 * 2 * MAIN * rows * width, bytes_accessed=12 * rows * width, transcendentals=0
        ),
        name="pack_lead",
    )(*arrays)
    rest = local_call(
        functools.partial(trail_kernel, n_pipe),
        "pack_trail",
        (lead, *trail),
        (payload,) * 3,
        flops=4 * 2 * MAIN * rows * width,
    )
    return (lead, *rest)


def activate(payloads, w_ref):
    count, width = len(payloads), w_ref.shape[0]
    seg = width // SEGS
    size = count * 2 * SEGS
    tails = jnp.concatenate([p[:, width : width + seg] for p in payloads], axis=0)
    row = lax.broadcasted_iota(jnp.int32, (size, size), 0)
    col = lax.broadcasted_iota(jnp.int32, (size, size), 1)
    order = ((row % count) * (2 * SEGS) + row // count == col).astype(jnp.bfloat16)
    tails = jnp.dot(order, tails, preferred_element_type=jnp.float32)
    x_tail, y_tail = (
        jnp.concatenate(
            [tails[s * count : (s + 1) * count] for s in range(first, first + SEGS)], axis=1
        ).astype(jnp.bfloat16)
        for first in (0, SEGS)
    )
    rows_x = jnp.concatenate([p[:, :width] for p in payloads] + [x_tail], axis=0)
    hidden = jnp.dot(rows_x, w_ref[...], preferred_element_type=jnp.float32)
    return (hidden * jax.nn.sigmoid(hidden)).astype(jnp.bfloat16), y_tail


def times(active, rows_y):
    return lax.dot_general(
        active, rows_y, (((0,), (0,)), ((), ())), preferred_element_type=jnp.float32
    )


def part_kernel(count, *refs):
    payloads, (w_ref, out_ref) = refs[:count], refs[count:]
    width = w_ref.shape[0]
    seg = width // SEGS
    active, y_tail = activate(payloads, w_ref)
    for s in range(SEGS):
        here = slice(s * seg, (s + 1) * seg)
        there = slice(width + (s + 1) * seg, width + (s + 2) * seg)
        rows_y = jnp.concatenate([p[:, there] for p in payloads] + [y_tail[:, here]], axis=0)
        out_ref[:, here] = times(active, rows_y)


def active_kernel(count, *refs):
    payloads, (w_ref, *before, active_ref, tail_ref) = refs[:count], refs[count:]
    active, tail = activate(payloads, w_ref)
    if before:
        mains = before[0].shape[0] // CAP * MAIN
        first, second = before[0][...].astype(jnp.float32), active.astype(jnp.float32)
        active = jnp.concatenate(
            [first[:mains], second[: count * MAIN], first[mains:], second[count * MAIN :]], axis=0
        ).astype(jnp.bfloat16)
        tail = jnp.concatenate(
            [before[1][...].astype(jnp.float32), tail.astype(jnp.float32)], axis=0
        ).astype(jnp.bfloat16)
    active_ref[...], tail_ref[...] = active, tail


def sum_kernel(count, offsets, *refs):
    blocks, (active_ref, tail_ref, before, out_ref, made, sems) = refs[:count], refs[count:]
    seg = tail_ref.shape[1] // SEGS
    active = active_ref[...]
    copies = []
    for s in range(SEGS):
        here = slice(s * seg, (s + 1) * seg)
        rows_y = [b[:, o + s * seg : o + (s + 1) * seg] for b, o in zip(blocks, offsets)]
        rows_y = jnp.concatenate(rows_y + [tail_ref[:, here]], axis=0)
        made[:, here] = (before[:, here] + times(active, rows_y)).astype(jnp.bfloat16)
        copies.append(
            pltpu.make_async_copy(made.at[:, here], out_ref.at[:, here], sems.at[0])
        )
        copies[-1].start()
    pltpu.make_async_copy(made, out_ref, sems.at[0]).wait()


def local_call(kernel, name, operands, outs, scratch=(), flops=0):
    specs = tuple(
        pl.BlockSpec(
            memory_space=pltpu.HBM if isinstance(out, jax.ShapeDtypeStruct) else pltpu.VMEM
        )
        for out in outs
    )
    return pl.pallas_call(
        kernel,
        out_shape=outs,
        in_specs=[pl.BlockSpec(memory_space=pltpu.VMEM)] * len(operands),
        out_specs=specs,
        scratch_shapes=scratch,
        compiler_params=pltpu.CompilerParams(vmem_limit_bytes=40 * 2**20),
        cost_estimate=pl.CostEstimate(
            flops=flops, bytes_accessed=sum(o.size * o.dtype.itemsize for o in operands),
            transcendentals=0,
        ),
        name=name,
    )(*operands)


def grad(got, firsts, seconds, weight_in):
    width, hidden = weight_in.shape
    count, late = len(got), len(seconds)
    (before,) = local_call(
        functools.partial(part_kernel, count),
        "grad_part",
        (*got, weight_in),
        (pltpu.VMEM((hidden, width), jnp.float32),),
        flops=4 * CAP * count * width * hidden,
    )
    done, ready = (), 0
    for group in firsts:
        ready += len(group)
        done = local_call(
            functools.partial(active_kernel, len(group)),
            "active_late",
            (*group, weight_in, *done),
            (
                pltpu.VMEM((ready * CAP, hidden), jnp.bfloat16),
                pltpu.VMEM((ready, width), jnp.bfloat16),
            ),
            flops=2 * CAP * len(group) * width * hidden,
        )
    active, tail = done
    (total,) = local_call(
        functools.partial(sum_kernel, late, [b.shape[1] - width for b in seconds]),
        "grad_sum",
        (*seconds, active, tail, before),
        (jax.ShapeDtypeStruct((hidden, width), jnp.bfloat16),),
        scratch=[pltpu.VMEM((hidden, width), jnp.bfloat16), pltpu.SemaphoreType.DMA((SEGS,))],
        flops=2 * CAP * late * width * hidden,
    )
    return total


def gather_both(lead, trail, up, n_pipe, cycle, cut):
    n = len(cycle)
    right = [(cycle[i], cycle[(i + 1) % n]) for i in range(n)]
    left = [(b, a) for a, b in right]

    def move(block, moves, mirrored=lambda turned: False):
        pairs = []
        for p in range(n_pipe):
            turned = is_turned(p, n_pipe)
            to = n_pipe - 1 - p if mirrored(turned) else p
            pairs += [(p * n + (b if turned else a), to * n + (a if turned else b)) for a, b in moves]
        return lax.ppermute(block, ("pipe", "expert"), pairs)

    def turn(at):
        return (move(at[0], left), move(at[1], right), move(at[2], right), move(at[3], left))

    at = (
        move(lead, left, lambda turned: not turned),
        move(trail, right, lambda turned: turned),
        move(lead, right, lambda turned: not turned),
        move(trail, left, lambda turned: turned),
    )
    got = [*at]
    for _ in range(1, (n - 1) // 2):
        at = turn(at)
        got += at
    whole = move(at[0], left)
    firsts = ((at[2], whole), (move(at[1][:, :cut], right),))
    seconds = (at[2], whole, move(at[1][:, cut:], right))
    own = move(up, [(e, e) for e in range(n)], lambda turned: True)
    return [*reversed(got[:-2]), got[-1], own], firsts, seconds


def body(
    tokens_down,
    cotan_down,
    gates_down,
    experts_down,
    tokens_up,
    cotan_up,
    gates_up,
    experts_up,
    w_in,
):
    n_pipe, n_expert = lax.axis_size("pipe"), lax.axis_size("expert")
    lead, trail, up, down = pack(
        (
            *(tokens_down[0], cotan_down[0], gates_down[0].T, experts_down[0].T),
            *(tokens_up[0], cotan_up[0], gates_up[0].T, experts_up[0].T),
        ),
        n_pipe,
    )
    width = w_in.shape[1]
    cut = width + width // SEGS
    got, firsts, seconds = gather_both(lead, trail, up, n_pipe, grid_cycle(n_expert), cut)
    return grad([*got, down], firsts, seconds, w_in[0])[None]


def solution(mesh):
    rows = P("pipe", "expert", None)
    in_specs = (rows,) * 8 + (P("pipe", None, "expert"),)
    return jax.shard_map(body, mesh=mesh, in_specs=in_specs, out_specs=rows, check_vma=False)
```

```python
import functools

import jax
import jax.numpy as jnp
from jax import lax
from jax.experimental import pallas as pl
from jax.experimental.pallas import tpu as pltpu
from jax.sharding import PartitionSpec as P

CAP = 17
MAIN = 16
SEGS = 8


def grid_cycle(n):
    fast = 1
    while 4 * fast * fast <= n:
        fast *= 2
    slow = n // fast
    order = [s * fast for s in range(slow)]
    for s in reversed(range(slow)):
        columns = range(1, fast)
        if (slow - 1 - s) % 2 == 1:
            columns = reversed(columns)
        order += [s * fast + c for c in columns]
    return order


def place(gates, ids):
    rows = ids.shape[1]
    named = ids == 0
    gate = jnp.sum(jnp.where(named, gates.astype(jnp.float32), 0.0), axis=0, keepdims=True)
    chosen = jnp.sum(named.astype(jnp.float32), axis=0, keepdims=True)
    earlier = (
        lax.broadcasted_iota(jnp.int32, (rows, rows), 0)
        < lax.broadcasted_iota(jnp.int32, (rows, rows), 1)
    ).astype(jnp.float32)
    slot = jnp.dot(
        jnp.broadcast_to(chosen, (8, rows)), earlier, preferred_element_type=jnp.float32
    )[:1].astype(jnp.int32)
    want = lax.broadcasted_iota(jnp.int32, (2 * MAIN, rows), 0)
    hit = (want == slot) & (chosen > 0.0) & (want < CAP)
    slot_gate = jnp.sum(jnp.where(hit, gate, 0.0), axis=1, keepdims=True)
    return hit.astype(jnp.bfloat16), slot_gate


def is_turned(p, n_pipe):
    return p % 2 != 2 * p // n_pipe


def write_payload(out_ref, tokens_ref, cotan_ref, placing, slot_gate):
    width = tokens_ref.shape[1]
    seg = width // SEGS
    x = jnp.dot(placing, tokens_ref[...], preferred_element_type=jnp.float32)
    y = jnp.dot(placing, cotan_ref[...], preferred_element_type=jnp.float32) * slot_gate
    out_ref[:, :width] = x[:MAIN].astype(jnp.bfloat16)
    out_ref[:, width + seg :] = y[:MAIN].astype(jnp.bfloat16)
    tail = [x[MAIN : MAIN + 1, s * seg : (s + 1) * seg] for s in range(SEGS)]
    tail += [y[MAIN : MAIN + 1, s * seg : (s + 1) * seg] for s in range(SEGS)]
    out_ref[:, width : width + seg] = jnp.concatenate(tail, axis=0).astype(jnp.bfloat16)


def lead_kernel(n_pipe, *refs):
    hbm, lead, trail, (tokens_ref, cotan_ref, gates_ref, ids_ref, sems) = (
        refs[:8],
        refs[8],
        refs[9:13],
        refs[13:],
    )
    held = (tokens_ref, cotan_ref, gates_ref, ids_ref, *trail)
    order = (2, 3, 0, 1, 6, 7, 4, 5)
    turned = is_turned(lax.axis_index("pipe"), n_pipe)

    def copies(swapped):
        sources = hbm[:4] + hbm[4:] if swapped else hbm[4:] + hbm[:4]
        return {i: pltpu.make_async_copy(sources[i], held[i], sems.at[i]) for i in order}

    for swapped in (False, True):

        @pl.when(turned == swapped)
        def _():
            for copy in copies(swapped).values():
                copy.start()

    waits = copies(False)
    waits[2].wait()
    waits[3].wait()
    placed = place(gates_ref[...], ids_ref[...])
    waits[0].wait()
    waits[1].wait()
    write_payload(lead, tokens_ref, cotan_ref, *placed)
    for i in range(4, 8):
        waits[i].wait()


def trail_kernel(n_pipe, lead, tokens_ref, cotan_ref, gates_ref, ids_ref, trail, up, down):
    write_payload(trail, tokens_ref, cotan_ref, *place(gates_ref[...], ids_ref[...]))
    turned = is_turned(lax.axis_index("pipe"), n_pipe)
    for swapped, first, second in ((False, up, down), (True, down, up)):

        @pl.when(turned == swapped)
        def _():
            first[...] = lead[...]
            second[...] = trail[...]


def pack(arrays, n_pipe):
    rows, width = arrays[0].shape
    seg = width // SEGS
    payload = pltpu.VMEM((MAIN, 2 * width + seg), jnp.bfloat16)
    arrays = [pltpu.with_memory_space_constraint(a, pltpu.HBM) for a in arrays]
    lead, *trail = pl.pallas_call(
        functools.partial(lead_kernel, n_pipe),
        out_shape=(payload, *(pltpu.VMEM(a.shape, a.dtype) for a in arrays[:4])),
        in_specs=[pl.BlockSpec(memory_space=pltpu.HBM)] * 8,
        out_specs=(pl.BlockSpec(memory_space=pltpu.VMEM),) * 5,
        scratch_shapes=[pltpu.VMEM(a.shape, a.dtype) for a in arrays[:4]]
        + [pltpu.SemaphoreType.DMA((8,))],
        compiler_params=pltpu.CompilerParams(vmem_limit_bytes=16 * 2**20),
        cost_estimate=pl.CostEstimate(
            flops=4 * 2 * MAIN * rows * width, bytes_accessed=12 * rows * width, transcendentals=0
        ),
        name="pack_lead",
    )(*arrays)
    rest = local_call(
        functools.partial(trail_kernel, n_pipe),
        "pack_trail",
        (lead, *trail),
        (payload,) * 3,
        flops=4 * 2 * MAIN * rows * width,
    )
    return (lead, *rest)


def activate(payloads, w_ref):
    count, width = len(payloads), w_ref.shape[0]
    seg = width // SEGS
    size = count * 2 * SEGS
    tails = jnp.concatenate([p[:, width : width + seg] for p in payloads], axis=0)
    row = lax.broadcasted_iota(jnp.int32, (size, size), 0)
    col = lax.broadcasted_iota(jnp.int32, (size, size), 1)
    order = ((row % count) * (2 * SEGS) + row // count == col).astype(jnp.bfloat16)
    tails = jnp.dot(order, tails, preferred_element_type=jnp.float32)
    x_tail, y_tail = (
        jnp.concatenate(
            [tails[s * count : (s + 1) * count] for s in range(first, first + SEGS)], axis=1
        ).astype(jnp.bfloat16)
        for first in (0, SEGS)
    )
    rows_x = jnp.concatenate([p[:, :width] for p in payloads] + [x_tail], axis=0)
    hidden = jnp.dot(rows_x, w_ref[...], preferred_element_type=jnp.float32)
    return (hidden * jax.nn.sigmoid(hidden)).astype(jnp.bfloat16), y_tail


def times(active, rows_y):
    return lax.dot_general(
        active, rows_y, (((0,), (0,)), ((), ())), preferred_element_type=jnp.float32
    )


def part_kernel(count, *refs):
    payloads, (w_ref, out_ref) = refs[:count], refs[count:]
    width = w_ref.shape[0]
    seg = width // SEGS
    active, y_tail = activate(payloads, w_ref)
    for s in range(SEGS):
        here = slice(s * seg, (s + 1) * seg)
        there = slice(width + (s + 1) * seg, width + (s + 2) * seg)
        rows_y = jnp.concatenate([p[:, there] for p in payloads] + [y_tail[:, here]], axis=0)
        out_ref[:, here] = times(active, rows_y)


def active_kernel(count, *refs):
    payloads, (w_ref, *before, active_ref, tail_ref) = refs[:count], refs[count:]
    active, tail = activate(payloads, w_ref)
    if before:
        mains = before[0].shape[0] // CAP * MAIN
        first, second = before[0][...].astype(jnp.float32), active.astype(jnp.float32)
        active = jnp.concatenate(
            [first[:mains], second[: count * MAIN], first[mains:], second[count * MAIN :]], axis=0
        ).astype(jnp.bfloat16)
        tail = jnp.concatenate(
            [before[1][...].astype(jnp.float32), tail.astype(jnp.float32)], axis=0
        ).astype(jnp.bfloat16)
    active_ref[...], tail_ref[...] = active, tail


def sum_kernel(count, offsets, *refs):
    blocks, (active_ref, tail_ref, before, out_ref, made, sems) = refs[:count], refs[count:]
    seg = tail_ref.shape[1] // SEGS
    active = active_ref[...]
    copies = []
    for s in range(SEGS):
        here = slice(s * seg, (s + 1) * seg)
        rows_y = [b[:, o + s * seg : o + (s + 1) * seg] for b, o in zip(blocks, offsets)]
        rows_y = jnp.concatenate(rows_y + [tail_ref[:, here]], axis=0)
        made[:, here] = (before[:, here] + times(active, rows_y)).astype(jnp.bfloat16)
        copies.append(
            pltpu.make_async_copy(made.at[:, here], out_ref.at[:, here], sems.at[0])
        )
        copies[-1].start()
    pltpu.make_async_copy(made, out_ref, sems.at[0]).wait()


def local_call(kernel, name, operands, outs, scratch=(), flops=0):
    specs = tuple(
        pl.BlockSpec(
            memory_space=pltpu.HBM if isinstance(out, jax.ShapeDtypeStruct) else pltpu.VMEM
        )
        for out in outs
    )
    return pl.pallas_call(
        kernel,
        out_shape=outs,
        in_specs=[pl.BlockSpec(memory_space=pltpu.VMEM)] * len(operands),
        out_specs=specs,
        scratch_shapes=scratch,
        compiler_params=pltpu.CompilerParams(vmem_limit_bytes=40 * 2**20),
        cost_estimate=pl.CostEstimate(
            flops=flops, bytes_accessed=sum(o.size * o.dtype.itemsize for o in operands),
            transcendentals=0,
        ),
        name=name,
    )(*operands)


def fetch_kernel(source, out_ref, sem):
    copy = pltpu.make_async_copy(source, out_ref, sem)
    copy.start()
    copy.wait()


def fetch(weight_in):
    return pl.pallas_call(
        fetch_kernel,
        out_shape=pltpu.VMEM(weight_in.shape, weight_in.dtype),
        in_specs=[pl.BlockSpec(memory_space=pltpu.HBM)],
        out_specs=pl.BlockSpec(memory_space=pltpu.VMEM),
        scratch_shapes=[pltpu.SemaphoreType.DMA],
        compiler_params=pltpu.CompilerParams(vmem_limit_bytes=16 * 2**20),
        name="fetch_weights",
    )(pltpu.with_memory_space_constraint(weight_in, pltpu.HBM))


def grad(got, firsts, seconds, weight_in):
    width, hidden = weight_in.shape
    count, late = len(got), len(seconds)
    (before,) = local_call(
        functools.partial(part_kernel, count),
        "grad_part",
        (*got, weight_in),
        (pltpu.VMEM((hidden, width), jnp.float32),),
        flops=4 * CAP * count * width * hidden,
    )
    done, ready = (), 0
    for group in firsts:
        ready += len(group)
        done = local_call(
            functools.partial(active_kernel, len(group)),
            "active_late",
            (*group, weight_in, *done),
            (
                pltpu.VMEM((ready * CAP, hidden), jnp.bfloat16),
                pltpu.VMEM((ready, width), jnp.bfloat16),
            ),
            flops=2 * CAP * len(group) * width * hidden,
        )
    active, tail = done
    (total,) = local_call(
        functools.partial(sum_kernel, late, [b.shape[1] - width for b in seconds]),
        "grad_sum",
        (*seconds, active, tail, before),
        (jax.ShapeDtypeStruct((hidden, width), jnp.bfloat16),),
        scratch=[pltpu.VMEM((hidden, width), jnp.bfloat16), pltpu.SemaphoreType.DMA((SEGS,))],
        flops=2 * CAP * late * width * hidden,
    )
    return total


def gather_both(lead, trail, up, held, n_pipe, cycle, cut):
    n = len(cycle)
    right = [(cycle[i], cycle[(i + 1) % n]) for i in range(n)]
    left = [(b, a) for a, b in right]

    def move(block, moves, mirrored=lambda turned: False):
        pairs = []
        for p in range(n_pipe):
            turned = is_turned(p, n_pipe)
            to = n_pipe - 1 - p if mirrored(turned) else p
            pairs += [(p * n + (b if turned else a), to * n + (a if turned else b)) for a, b in moves]
        return lax.ppermute(block, ("pipe", "expert"), pairs)

    def turn(at):
        return (move(at[0], left), move(at[1], right), move(at[2], right), move(at[3], left))

    at = (
        move(lead, left, lambda turned: not turned),
        move(trail, right, lambda turned: turned),
        move(lead, right, lambda turned: not turned),
        move(trail, left, lambda turned: turned),
    )
    got = [*at]
    first, held = lax.optimization_barrier((at[0], held))
    at = (first, *at[1:])
    for _ in range(1, (n - 1) // 2):
        at = turn(at)
        got += at
    whole = move(at[0], left)
    firsts = ((at[2], whole), (move(at[1][:, :cut], right),))
    seconds = (at[2], whole, move(at[1][:, cut:], right))
    own = move(up, [(e, e) for e in range(n)], lambda turned: True)
    return [*reversed(got[:-2]), got[-1], own], firsts, seconds


def body(
    tokens_down,
    cotan_down,
    gates_down,
    experts_down,
    tokens_up,
    cotan_up,
    gates_up,
    experts_up,
    w_in,
):
    n_pipe, n_expert = lax.axis_size("pipe"), lax.axis_size("expert")
    lead, trail, up, down = pack(
        (
            *(tokens_down[0], cotan_down[0], gates_down[0].T, experts_down[0].T),
            *(tokens_up[0], cotan_up[0], gates_up[0].T, experts_up[0].T),
        ),
        n_pipe,
    )
    width = w_in.shape[1]
    cut = width + width // SEGS
    weight_in = fetch(w_in[0])
    got, firsts, seconds = gather_both(lead, trail, up, weight_in, n_pipe, grid_cycle(n_expert), cut)
    return grad([*got, down], firsts, seconds, weight_in)[None]


def solution(mesh):
    rows = P("pipe", "expert", None)
    in_specs = (rows,) * 8 + (P("pipe", None, "expert"),)
    return jax.shard_map(body, mesh=mesh, in_specs=in_specs, out_specs=rows, check_vma=False)
```

```python
import functools

import jax
import jax.numpy as jnp
from jax import lax
from jax.experimental import pallas as pl
from jax.experimental.pallas import tpu as pltpu
from jax.sharding import PartitionSpec as P

CAP = 17
MAIN = 16
SEGS = 8


def grid_cycle(n):
    fast = 1
    while 4 * fast * fast <= n:
        fast *= 2
    slow = n // fast
    order = [s * fast for s in range(slow)]
    for s in reversed(range(slow)):
        columns = range(1, fast)
        if (slow - 1 - s) % 2 == 1:
            columns = reversed(columns)
        order += [s * fast + c for c in columns]
    return order


def place(gates, ids):
    rows = ids.shape[1]
    named = ids == 0
    gate = jnp.sum(jnp.where(named, gates.astype(jnp.float32), 0.0), axis=0, keepdims=True)
    chosen = jnp.sum(named.astype(jnp.float32), axis=0, keepdims=True)
    earlier = (
        lax.broadcasted_iota(jnp.int32, (rows, rows), 0)
        < lax.broadcasted_iota(jnp.int32, (rows, rows), 1)
    ).astype(jnp.float32)
    slot = jnp.dot(
        jnp.broadcast_to(chosen, (8, rows)), earlier, preferred_element_type=jnp.float32
    )[:1].astype(jnp.int32)
    want = lax.broadcasted_iota(jnp.int32, (2 * MAIN, rows), 0)
    hit = (want == slot) & (chosen > 0.0) & (want < CAP)
    slot_gate = jnp.sum(jnp.where(hit, gate, 0.0), axis=1, keepdims=True)
    return hit.astype(jnp.bfloat16), slot_gate


def is_turned(p, n_pipe):
    return p % 2 != 2 * p // n_pipe


def write_payload(out_ref, tokens_ref, cotan_ref, placing, slot_gate):
    width = tokens_ref.shape[1]
    seg = width // SEGS
    x = jnp.dot(placing, tokens_ref[...], preferred_element_type=jnp.float32)
    y = jnp.dot(placing, cotan_ref[...], preferred_element_type=jnp.float32) * slot_gate
    out_ref[:, :width] = x[:MAIN].astype(jnp.bfloat16)
    out_ref[:, width + seg :] = y[:MAIN].astype(jnp.bfloat16)
    tail = [x[MAIN : MAIN + 1, s * seg : (s + 1) * seg] for s in range(SEGS)]
    tail += [y[MAIN : MAIN + 1, s * seg : (s + 1) * seg] for s in range(SEGS)]
    out_ref[:, width : width + seg] = jnp.concatenate(tail, axis=0).astype(jnp.bfloat16)


def lead_kernel(n_pipe, *refs):
    hbm, lead, trail, (tokens_ref, cotan_ref, gates_ref, ids_ref, sems) = (
        refs[:8],
        refs[8],
        refs[9:13],
        refs[13:],
    )
    held = (tokens_ref, cotan_ref, gates_ref, ids_ref, *trail)
    order = (2, 3, 0, 1, 6, 7, 4, 5)
    turned = is_turned(lax.axis_index("pipe"), n_pipe)

    def copies(swapped):
        sources = hbm[:4] + hbm[4:] if swapped else hbm[4:] + hbm[:4]
        return {i: pltpu.make_async_copy(sources[i], held[i], sems.at[i]) for i in order}

    for swapped in (False, True):

        @pl.when(turned == swapped)
        def _():
            for copy in copies(swapped).values():
                copy.start()

    waits = copies(False)
    waits[2].wait()
    waits[3].wait()
    placed = place(gates_ref[...], ids_ref[...])
    waits[0].wait()
    waits[1].wait()
    write_payload(lead, tokens_ref, cotan_ref, *placed)
    for i in range(4, 8):
        waits[i].wait()


def trail_kernel(tokens_ref, cotan_ref, gates_ref, ids_ref, trail):
    write_payload(trail, tokens_ref, cotan_ref, *place(gates_ref[...], ids_ref[...]))


def pack(arrays, n_pipe):
    rows, width = arrays[0].shape
    seg = width // SEGS
    payload = pltpu.VMEM((MAIN, 2 * width + seg), jnp.bfloat16)
    arrays = [pltpu.with_memory_space_constraint(a, pltpu.HBM) for a in arrays]
    lead, *trail = pl.pallas_call(
        functools.partial(lead_kernel, n_pipe),
        out_shape=(payload, *(pltpu.VMEM(a.shape, a.dtype) for a in arrays[:4])),
        in_specs=[pl.BlockSpec(memory_space=pltpu.HBM)] * 8,
        out_specs=(pl.BlockSpec(memory_space=pltpu.VMEM),) * 5,
        scratch_shapes=[pltpu.VMEM(a.shape, a.dtype) for a in arrays[:4]]
        + [pltpu.SemaphoreType.DMA((8,))],
        compiler_params=pltpu.CompilerParams(vmem_limit_bytes=16 * 2**20),
        cost_estimate=pl.CostEstimate(
            flops=4 * 2 * MAIN * rows * width, bytes_accessed=12 * rows * width, transcendentals=0
        ),
        name="pack_lead",
    )(*arrays)
    (rest,) = local_call(
        trail_kernel,
        "pack_trail",
        tuple(trail),
        (payload,),
        flops=4 * 2 * MAIN * rows * width,
    )
    return lead, rest


def activate(payloads, w_ref):
    count, width = len(payloads), w_ref.shape[0]
    seg = width // SEGS
    size = count * 2 * SEGS
    tails = jnp.concatenate([p[:, width : width + seg] for p in payloads], axis=0)
    row = lax.broadcasted_iota(jnp.int32, (size, size), 0)
    col = lax.broadcasted_iota(jnp.int32, (size, size), 1)
    order = ((row % count) * (2 * SEGS) + row // count == col).astype(jnp.bfloat16)
    tails = jnp.dot(order, tails, preferred_element_type=jnp.float32)
    x_tail, y_tail = (
        jnp.concatenate(
            [tails[s * count : (s + 1) * count] for s in range(first, first + SEGS)], axis=1
        ).astype(jnp.bfloat16)
        for first in (0, SEGS)
    )
    rows_x = jnp.concatenate([p[:, :width] for p in payloads] + [x_tail], axis=0)
    hidden = jnp.dot(rows_x, w_ref[...], preferred_element_type=jnp.float32)
    return (hidden * jax.nn.sigmoid(hidden)).astype(jnp.bfloat16), y_tail


def times(active, rows_y):
    return lax.dot_general(
        active, rows_y, (((0,), (0,)), ((), ())), preferred_element_type=jnp.float32
    )


def part_kernel(count, *refs):
    payloads, (w_ref, out_ref) = refs[:count], refs[count:]
    width = w_ref.shape[0]
    seg = width // SEGS
    active, y_tail = activate(payloads, w_ref)
    for s in range(SEGS):
        here = slice(s * seg, (s + 1) * seg)
        there = slice(width + (s + 1) * seg, width + (s + 2) * seg)
        rows_y = jnp.concatenate([p[:, there] for p in payloads] + [y_tail[:, here]], axis=0)
        out_ref[:, here] = times(active, rows_y)


def active_kernel(count, *refs):
    payloads, (w_ref, *before, active_ref, tail_ref) = refs[:count], refs[count:]
    active, tail = activate(payloads, w_ref)
    if before:
        mains = before[0].shape[0] // CAP * MAIN
        first, second = before[0][...].astype(jnp.float32), active.astype(jnp.float32)
        active = jnp.concatenate(
            [first[:mains], second[: count * MAIN], first[mains:], second[count * MAIN :]], axis=0
        ).astype(jnp.bfloat16)
        tail = jnp.concatenate(
            [before[1][...].astype(jnp.float32), tail.astype(jnp.float32)], axis=0
        ).astype(jnp.bfloat16)
    active_ref[...], tail_ref[...] = active, tail


def sum_kernel(count, offsets, *refs):
    blocks, (active_ref, tail_ref, before, out_ref, made, sems) = refs[:count], refs[count:]
    seg = tail_ref.shape[1] // SEGS
    active = active_ref[...]
    copies = []
    for s in range(SEGS):
        here = slice(s * seg, (s + 1) * seg)
        rows_y = [b[:, o + s * seg : o + (s + 1) * seg] for b, o in zip(blocks, offsets)]
        rows_y = jnp.concatenate(rows_y + [tail_ref[:, here]], axis=0)
        made[:, here] = (before[:, here] + times(active, rows_y)).astype(jnp.bfloat16)
        copies.append(
            pltpu.make_async_copy(made.at[:, here], out_ref.at[:, here], sems.at[0])
        )
        copies[-1].start()
    pltpu.make_async_copy(made, out_ref, sems.at[0]).wait()


def local_call(kernel, name, operands, outs, scratch=(), flops=0):
    specs = tuple(
        pl.BlockSpec(
            memory_space=pltpu.HBM if isinstance(out, jax.ShapeDtypeStruct) else pltpu.VMEM
        )
        for out in outs
    )
    return pl.pallas_call(
        kernel,
        out_shape=outs,
        in_specs=[pl.BlockSpec(memory_space=pltpu.VMEM)] * len(operands),
        out_specs=specs,
        scratch_shapes=scratch,
        compiler_params=pltpu.CompilerParams(vmem_limit_bytes=40 * 2**20),
        cost_estimate=pl.CostEstimate(
            flops=flops, bytes_accessed=sum(o.size * o.dtype.itemsize for o in operands),
            transcendentals=0,
        ),
        name=name,
    )(*operands)


def fetch_kernel(n_pipe, source, lead, trail, weights, up, down, sem):
    copy = pltpu.make_async_copy(source, weights, sem)
    copy.start()
    turned = is_turned(lax.axis_index("pipe"), n_pipe)
    for swapped, first, second in ((False, up, down), (True, down, up)):

        @pl.when(turned == swapped)
        def _():
            first[...] = lead[...]
            second[...] = trail[...]
    copy.wait()


def fetch(weight_in, lead, trail, n_pipe):
    payload = pltpu.VMEM(lead.shape, lead.dtype)
    vmem = pl.BlockSpec(memory_space=pltpu.VMEM)
    return pl.pallas_call(
        functools.partial(fetch_kernel, n_pipe),
        out_shape=(pltpu.VMEM(weight_in.shape, weight_in.dtype), payload, payload),
        in_specs=[pl.BlockSpec(memory_space=pltpu.HBM), vmem, vmem],
        out_specs=(vmem,) * 3,
        scratch_shapes=[pltpu.SemaphoreType.DMA],
        compiler_params=pltpu.CompilerParams(vmem_limit_bytes=16 * 2**20),
        name="fetch_weights",
    )(pltpu.with_memory_space_constraint(weight_in, pltpu.HBM), lead, trail)


def grad(got, firsts, seconds, weight_in):
    width, hidden = weight_in.shape
    count, late = len(got), len(seconds)
    (before,) = local_call(
        functools.partial(part_kernel, count),
        "grad_part",
        (*got, weight_in),
        (pltpu.VMEM((hidden, width), jnp.float32),),
        flops=4 * CAP * count * width * hidden,
    )
    done, ready = (), 0
    for group in firsts:
        ready += len(group)
        done = local_call(
            functools.partial(active_kernel, len(group)),
            "active_late",
            (*group, weight_in, *done),
            (
                pltpu.VMEM((ready * CAP, hidden), jnp.bfloat16),
                pltpu.VMEM((ready, width), jnp.bfloat16),
            ),
            flops=2 * CAP * len(group) * width * hidden,
        )
    active, tail = done
    (total,) = local_call(
        functools.partial(sum_kernel, late, [b.shape[1] - width for b in seconds]),
        "grad_sum",
        (*seconds, active, tail, before),
        (jax.ShapeDtypeStruct((hidden, width), jnp.bfloat16),),
        scratch=[pltpu.VMEM((hidden, width), jnp.bfloat16), pltpu.SemaphoreType.DMA((SEGS,))],
        flops=2 * CAP * late * width * hidden,
    )
    return total


def gather_both(lead, trail, up, held, n_pipe, cycle, cut):
    n = len(cycle)
    right = [(cycle[i], cycle[(i + 1) % n]) for i in range(n)]
    left = [(b, a) for a, b in right]

    def move(block, moves, mirrored=lambda turned: False):
        pairs = []
        for p in range(n_pipe):
            turned = is_turned(p, n_pipe)
            to = n_pipe - 1 - p if mirrored(turned) else p
            pairs += [(p * n + (b if turned else a), to * n + (a if turned else b)) for a, b in moves]
        return lax.ppermute(block, ("pipe", "expert"), pairs)

    def turn(at):
        return (move(at[0], left), move(at[1], right), move(at[2], right), move(at[3], left))

    at = (
        move(lead, left, lambda turned: not turned),
        move(trail, right, lambda turned: turned),
        move(lead, right, lambda turned: not turned),
        move(trail, left, lambda turned: turned),
    )
    got = [*at]
    first, held = lax.optimization_barrier((at[0], held))
    at = (first, *at[1:])
    for _ in range(1, (n - 1) // 2):
        at = turn(at)
        got += at
    whole = move(at[0], left)
    firsts = ((at[2], whole), (move(at[1][:, :cut], right),))
    seconds = (at[2], whole, move(at[1][:, cut:], right))
    own = move(up, [(e, e) for e in range(n)], lambda turned: True)
    return [*reversed(got[:-2]), got[-1], own], firsts, seconds


def body(
    tokens_down,
    cotan_down,
    gates_down,
    experts_down,
    tokens_up,
    cotan_up,
    gates_up,
    experts_up,
    w_in,
):
    n_pipe, n_expert = lax.axis_size("pipe"), lax.axis_size("expert")
    lead, trail = pack(
        (
            *(tokens_down[0], cotan_down[0], gates_down[0].T, experts_down[0].T),
            *(tokens_up[0], cotan_up[0], gates_up[0].T, experts_up[0].T),
        ),
        n_pipe,
    )
    width = w_in.shape[1]
    cut = width + width // SEGS
    weight_in, up, down = fetch(w_in[0], lead, trail, n_pipe)
    got, firsts, seconds = gather_both(lead, trail, up, weight_in, n_pipe, grid_cycle(n_expert), cut)
    return grad([*got, down], firsts, seconds, weight_in)[None]


def solution(mesh):
    rows = P("pipe", "expert", None)
    in_specs = (rows,) * 8 + (P("pipe", None, "expert"),)
    return jax.shard_map(body, mesh=mesh, in_specs=in_specs, out_specs=rows, check_vma=False)
```

```python
import functools

import jax
import jax.numpy as jnp
from jax import lax
from jax.experimental import pallas as pl
from jax.experimental.pallas import tpu as pltpu
from jax.sharding import PartitionSpec as P

CAP = 17
MAIN = 16
SEGS = 8
PIECES = 3


def grid_cycle(n):
    fast = 1
    while 4 * fast * fast <= n:
        fast *= 2
    slow = n // fast
    order = [s * fast for s in range(slow)]
    for s in reversed(range(slow)):
        columns = range(1, fast)
        if (slow - 1 - s) % 2 == 1:
            columns = reversed(columns)
        order += [s * fast + c for c in columns]
    return order


def place(gates, ids):
    rows = ids.shape[1]
    named = ids == 0
    gate = jnp.sum(jnp.where(named, gates.astype(jnp.float32), 0.0), axis=0, keepdims=True)
    chosen = jnp.sum(named.astype(jnp.float32), axis=0, keepdims=True)
    earlier = (
        lax.broadcasted_iota(jnp.int32, (rows, rows), 0)
        < lax.broadcasted_iota(jnp.int32, (rows, rows), 1)
    ).astype(jnp.float32)
    slot = jnp.dot(
        jnp.broadcast_to(chosen, (8, rows)), earlier, preferred_element_type=jnp.float32
    )[:1].astype(jnp.int32)
    want = lax.broadcasted_iota(jnp.int32, (2 * MAIN, rows), 0)
    hit = (want == slot) & (chosen > 0.0) & (want < CAP)
    slot_gate = jnp.sum(jnp.where(hit, gate, 0.0), axis=1, keepdims=True)
    return hit.astype(jnp.bfloat16), slot_gate


def is_turned(p, n_pipe):
    return p % 2 != 2 * p // n_pipe


def write_payload(out_ref, tokens_ref, cotan_ref, placing, slot_gate):
    width = tokens_ref.shape[1]
    seg = width // SEGS
    x = jnp.dot(placing, tokens_ref[...], preferred_element_type=jnp.float32)
    y = jnp.dot(placing, cotan_ref[...], preferred_element_type=jnp.float32) * slot_gate
    out_ref[:, :width] = x[:MAIN].astype(jnp.bfloat16)
    out_ref[:, width + seg :] = y[:MAIN].astype(jnp.bfloat16)
    tail = [x[MAIN : MAIN + 1, s * seg : (s + 1) * seg] for s in range(SEGS)]
    tail += [y[MAIN : MAIN + 1, s * seg : (s + 1) * seg] for s in range(SEGS)]
    out_ref[:, width : width + seg] = jnp.concatenate(tail, axis=0).astype(jnp.bfloat16)


def lead_kernel(n_pipe, *refs):
    hbm, lead, trail, (tokens_ref, cotan_ref, gates_ref, ids_ref, sems) = (
        refs[:8],
        refs[8],
        refs[9:13],
        refs[13:],
    )
    held = (tokens_ref, cotan_ref, gates_ref, ids_ref, *trail)
    order = (2, 3, 0, 1, 6, 7, 4, 5)
    turned = is_turned(lax.axis_index("pipe"), n_pipe)

    def copies(swapped):
        sources = hbm[:4] + hbm[4:] if swapped else hbm[4:] + hbm[:4]
        return {i: pltpu.make_async_copy(sources[i], held[i], sems.at[i]) for i in order}

    for swapped in (False, True):

        @pl.when(turned == swapped)
        def _():
            for copy in copies(swapped).values():
                copy.start()

    waits = copies(False)
    waits[2].wait()
    waits[3].wait()
    placed = place(gates_ref[...], ids_ref[...])
    waits[0].wait()
    waits[1].wait()
    write_payload(lead, tokens_ref, cotan_ref, *placed)
    for i in range(4, 8):
        waits[i].wait()


def trail_kernel(n_pipe, lead, tokens_ref, cotan_ref, gates_ref, ids_ref, trail, up, down):
    write_payload(trail, tokens_ref, cotan_ref, *place(gates_ref[...], ids_ref[...]))
    turned = is_turned(lax.axis_index("pipe"), n_pipe)
    for swapped, first, second in ((False, up, down), (True, down, up)):

        @pl.when(turned == swapped)
        def _():
            first[...] = lead[...]
            second[...] = trail[...]


def pack(arrays, n_pipe):
    rows, width = arrays[0].shape
    seg = width // SEGS
    payload = pltpu.VMEM((MAIN, 2 * width + seg), jnp.bfloat16)
    arrays = [pltpu.with_memory_space_constraint(a, pltpu.HBM) for a in arrays]
    lead, *trail = pl.pallas_call(
        functools.partial(lead_kernel, n_pipe),
        out_shape=(payload, *(pltpu.VMEM(a.shape, a.dtype) for a in arrays[:4])),
        in_specs=[pl.BlockSpec(memory_space=pltpu.HBM)] * 8,
        out_specs=(pl.BlockSpec(memory_space=pltpu.VMEM),) * 5,
        scratch_shapes=[pltpu.VMEM(a.shape, a.dtype) for a in arrays[:4]]
        + [pltpu.SemaphoreType.DMA((8,))],
        compiler_params=pltpu.CompilerParams(vmem_limit_bytes=16 * 2**20),
        cost_estimate=pl.CostEstimate(
            flops=4 * 2 * MAIN * rows * width, bytes_accessed=12 * rows * width, transcendentals=0
        ),
        name="pack_lead",
    )(*arrays)
    rest = local_call(
        functools.partial(trail_kernel, n_pipe),
        "pack_trail",
        (lead, *trail),
        (payload,) * 3,
        flops=4 * 2 * MAIN * rows * width,
    )
    return (lead, *rest)


def activate(payloads, w_ref):
    count, width = len(payloads), w_ref.shape[0]
    seg = width // SEGS
    size = count * 2 * SEGS
    tails = jnp.concatenate([p[:, width : width + seg] for p in payloads], axis=0)
    row = lax.broadcasted_iota(jnp.int32, (size, size), 0)
    col = lax.broadcasted_iota(jnp.int32, (size, size), 1)
    order = ((row % count) * (2 * SEGS) + row // count == col).astype(jnp.bfloat16)
    tails = jnp.dot(order, tails, preferred_element_type=jnp.float32)
    x_tail, y_tail = (
        jnp.concatenate(
            [tails[s * count : (s + 1) * count] for s in range(first, first + SEGS)], axis=1
        ).astype(jnp.bfloat16)
        for first in (0, SEGS)
    )
    rows_x = jnp.concatenate([p[:, :width] for p in payloads] + [x_tail], axis=0)
    hidden = jnp.dot(rows_x, w_ref[...], preferred_element_type=jnp.float32)
    return (hidden * jax.nn.sigmoid(hidden)).astype(jnp.bfloat16), y_tail


def times(active, rows_y):
    return lax.dot_general(
        active, rows_y, (((0,), (0,)), ((), ())), preferred_element_type=jnp.float32
    )


def part_kernel(count, *refs):
    payloads, (w_ref, out_ref) = refs[:count], refs[count:]
    width = w_ref.shape[0]
    seg = width // SEGS
    active, y_tail = activate(payloads, w_ref)
    for s in range(SEGS):
        here = slice(s * seg, (s + 1) * seg)
        there = slice(width + (s + 1) * seg, width + (s + 2) * seg)
        rows_y = jnp.concatenate([p[:, there] for p in payloads] + [y_tail[:, here]], axis=0)
        out_ref[:, here] = times(active, rows_y)


def active_kernel(count, *refs):
    payloads, (w_ref, *before, active_ref, tail_ref) = refs[:count], refs[count:]
    active, tail = activate(payloads, w_ref)
    if before:
        mains = before[0].shape[0] // CAP * MAIN
        first, second = before[0][...].astype(jnp.float32), active.astype(jnp.float32)
        active = jnp.concatenate(
            [first[:mains], second[: count * MAIN], first[mains:], second[count * MAIN :]], axis=0
        ).astype(jnp.bfloat16)
        tail = jnp.concatenate(
            [before[1][...].astype(jnp.float32), tail.astype(jnp.float32)], axis=0
        ).astype(jnp.bfloat16)
    active_ref[...], tail_ref[...] = active, tail


def sum_kernel(count, offsets, *refs):
    blocks, (active_ref, tail_ref, before, out_ref, made, sems) = refs[:count], refs[count:]
    seg = tail_ref.shape[1] // PIECES
    active = active_ref[...]
    copies = []
    for s in range(PIECES):
        here = slice(s * seg, (s + 1) * seg)
        rows_y = [b[:, o + s * seg : o + (s + 1) * seg] for b, o in zip(blocks, offsets)]
        rows_y = jnp.concatenate(rows_y + [tail_ref[:, here]], axis=0)
        made[:, here] = (before[:, here] + times(active, rows_y)).astype(jnp.bfloat16)
        copies.append(
            pltpu.make_async_copy(made.at[:, here], out_ref.at[:, here], sems.at[0])
        )
        copies[-1].start()
    pltpu.make_async_copy(made, out_ref, sems.at[0]).wait()


def local_call(kernel, name, operands, outs, scratch=(), flops=0):
    specs = tuple(
        pl.BlockSpec(
            memory_space=pltpu.HBM if isinstance(out, jax.ShapeDtypeStruct) else pltpu.VMEM
        )
        for out in outs
    )
    return pl.pallas_call(
        kernel,
        out_shape=outs,
        in_specs=[pl.BlockSpec(memory_space=pltpu.VMEM)] * len(operands),
        out_specs=specs,
        scratch_shapes=scratch,
        compiler_params=pltpu.CompilerParams(vmem_limit_bytes=40 * 2**20),
        cost_estimate=pl.CostEstimate(
            flops=flops, bytes_accessed=sum(o.size * o.dtype.itemsize for o in operands),
            transcendentals=0,
        ),
        name=name,
    )(*operands)


def fetch_kernel(source, out_ref, sem):
    copy = pltpu.make_async_copy(source, out_ref, sem)
    copy.start()
    copy.wait()


def fetch(weight_in):
    return pl.pallas_call(
        fetch_kernel,
        out_shape=pltpu.VMEM(weight_in.shape, weight_in.dtype),
        in_specs=[pl.BlockSpec(memory_space=pltpu.HBM)],
        out_specs=pl.BlockSpec(memory_space=pltpu.VMEM),
        scratch_shapes=[pltpu.SemaphoreType.DMA],
        compiler_params=pltpu.CompilerParams(vmem_limit_bytes=16 * 2**20),
        name="fetch_weights",
    )(pltpu.with_memory_space_constraint(weight_in, pltpu.HBM))


def grad(got, firsts, seconds, weight_in):
    width, hidden = weight_in.shape
    count, late = len(got), len(seconds)
    (before,) = local_call(
        functools.partial(part_kernel, count),
        "grad_part",
        (*got, weight_in),
        (pltpu.VMEM((hidden, width), jnp.float32),),
        flops=4 * CAP * count * width * hidden,
    )
    done, ready = (), 0
    for group in firsts:
        ready += len(group)
        done = local_call(
            functools.partial(active_kernel, len(group)),
            "active_late",
            (*group, weight_in, *done),
            (
                pltpu.VMEM((ready * CAP, hidden), jnp.bfloat16),
                pltpu.VMEM((ready, width), jnp.bfloat16),
            ),
            flops=2 * CAP * len(group) * width * hidden,
        )
    active, tail = done
    (total,) = local_call(
        functools.partial(sum_kernel, late, [b.shape[1] - width for b in seconds]),
        "grad_sum",
        (*seconds, active, tail, before),
        (jax.ShapeDtypeStruct((hidden, width), jnp.bfloat16),),
        scratch=[pltpu.VMEM((hidden, width), jnp.bfloat16), pltpu.SemaphoreType.DMA((SEGS,))],
        flops=2 * CAP * late * width * hidden,
    )
    return total


def gather_both(lead, trail, up, held, n_pipe, cycle, cut):
    n = len(cycle)
    right = [(cycle[i], cycle[(i + 1) % n]) for i in range(n)]
    left = [(b, a) for a, b in right]

    def move(block, moves, mirrored=lambda turned: False):
        pairs = []
        for p in range(n_pipe):
            turned = is_turned(p, n_pipe)
            to = n_pipe - 1 - p if mirrored(turned) else p
            pairs += [(p * n + (b if turned else a), to * n + (a if turned else b)) for a, b in moves]
        return lax.ppermute(block, ("pipe", "expert"), pairs)

    def turn(at):
        return (move(at[0], left), move(at[1], right), move(at[2], right), move(at[3], left))

    at = (
        move(lead, left, lambda turned: not turned),
        move(trail, right, lambda turned: turned),
        move(lead, right, lambda turned: not turned),
        move(trail, left, lambda turned: turned),
    )
    got = [*at]
    first, held = lax.optimization_barrier((at[0], held))
    at = (first, *at[1:])
    for _ in range(1, (n - 1) // 2):
        at = turn(at)
        got += at
    whole = move(at[0], left)
    firsts = ((at[2], whole), (move(at[1][:, :cut], right),))
    seconds = (at[2], whole, move(at[1][:, cut:], right))
    own = move(up, [(e, e) for e in range(n)], lambda turned: True)
    return [*reversed(got[:-2]), got[-1], own], firsts, seconds


def body(
    tokens_down,
    cotan_down,
    gates_down,
    experts_down,
    tokens_up,
    cotan_up,
    gates_up,
    experts_up,
    w_in,
):
    n_pipe, n_expert = lax.axis_size("pipe"), lax.axis_size("expert")
    lead, trail, up, down = pack(
        (
            *(tokens_down[0], cotan_down[0], gates_down[0].T, experts_down[0].T),
            *(tokens_up[0], cotan_up[0], gates_up[0].T, experts_up[0].T),
        ),
        n_pipe,
    )
    width = w_in.shape[1]
    cut = width + width // SEGS
    weight_in = fetch(w_in[0])
    got, firsts, seconds = gather_both(lead, trail, up, weight_in, n_pipe, grid_cycle(n_expert), cut)
    return grad([*got, down], firsts, seconds, weight_in)[None]


def solution(mesh):
    rows = P("pipe", "expert", None)
    in_specs = (rows,) * 8 + (P("pipe", None, "expert"),)
    return jax.shard_map(body, mesh=mesh, in_specs=in_specs, out_specs=rows, check_vma=False)
```
